256 devices in a mesh: gx: 32 (over x_lo, z, core), gy: 8 (over y, x_hi).
Axes of the slice: x: 4 (x_hi: 2, x_lo: 2; x = x_hi * 2 + x_lo), y: 4, z: 8, core: 2. Of those that a mesh axis runs over, the one named last changes fastest.
Arguments:
- ocean_state: float32 [4, 32, 1024, 1024], P(None, None, 'gx', 'gy'), may hold values from -6 to 6
- barotropic: float32 [3, 1024, 1024], P(None, 'gx', 'gy'), may hold values from -4 to 4
- levels: int32 [1024, 1024], P('gx', 'gy'), may hold values from 0 to 32, as said below
Outputs:
- new_ocean: float32 [4, 32, 1024, 1024], P(None, None, 'gx', 'gy')
- new_barotropic: float32 [3, 1024, 1024], P(None, 'gx', 'gy')
The draws below stay inside these ranges and needn't reach their ends.
Inputs may be any that keep to these rules, and one draw needn't show every extreme that they name: `levels`: the first and last meridional rows are land (0).
All inputs are finite; a program needn't handle non-finite values.
Results may differ from the reference program's by a relative error of at most 0.00002.
Values sent between devices are 32-bit elements; how exact they have to be, the bound alone decides.
A program may use at most 64 MiB of HBM per device.

```python
import jax
import jax.numpy as jnp

K = 32
NSUB = 16
NX = 1024
NY = 1024


def draw_levels(key, part):
    key = jax.random.fold_in(key, 7)
    key_land, key_depth = jax.random.split(key)
    blocks = jax.random.randint(key_land, (NX // 4, NY // 4), 0, 8)
    column = jnp.arange(NX // 4)[:, None]
    limit = 1 + 3 * column // (NX // 4)
    land = jnp.repeat(jnp.repeat(blocks < limit, 4, axis=0), 4, axis=1)
    depth = jax.random.randint(key_depth, (NX, NY), 1, K + 1)
    rows = jnp.arange(NY)[None, :]
    wall = (rows == 0) | (rows == NY - 1)
    return jnp.where(land | wall, 0, depth).astype(jnp.int32)


def shard_levels(stream_key, shape, pieces, least, high):
    loudness = 1.0
    for axis_at, shards_of in pieces:
        heights = jax.random.uniform(jax.random.fold_in(jax.random.fold_in(stream_key, 6), axis_at), (shards_of,), jnp.float32, least / len(pieces), high / len(pieces))
        loudness = loudness * jnp.repeat(jnp.exp(heights), shape[axis_at] // shards_of).reshape((-1,) + (1,) * (len(shape) - 1 - axis_at))
    return loudness


def normal_values(rng, shape, width, reach, pieces=(), kind=jnp.bfloat16):
    gain = shard_levels(rng, shape, pieces, -0.22, 0.18) if pieces else 1.0
    drawn = jax.random.normal(rng, shape, jnp.float32) * width * gain
    return jnp.minimum(jnp.maximum(drawn, -reach), reach).astype(kind)


def setup_inputs(seed: int = 0) -> dict:
    seeds = jax.random.split(jax.random.key(seed), 4)
    return {
        "ocean_state": normal_values(seeds[0], (4, K, NX, NY), 1.0, 6.0, ((2, 32), (3, 8)), jnp.float32),
        "barotropic": normal_values(seeds[1], (3, NX, NY), 0.5, 4.0, ((1, 32), (2, 8)), jnp.float32),
        "levels": draw_levels(jax.random.fold_in(seeds[3], 71), 0),
    }


def near(a):
    return (a, jnp.roll(a, -1, -2), jnp.roll(a, 1, -2), jnp.roll(a, -1, -1), jnp.roll(a, 1, -1))


def keep(a):
    return a


def baroclinic(ext, fcor, near_fn):
    u_all, v_all, t_all, s_all, m_all = ext[0], ext[1], ext[2], ext[3], ext[4]
    press = jnp.cumsum(m_all * (0.1 * s_all - 0.2 * t_all), axis=0)
    mc, me, mw, mn, ms = near_fn(m_all)

    def lapl(q):
        qc, qe, qw, qn, qs = near_fn(q)
        return mc * me * (qe - qc) + mc * mw * (qw - qc) + mc * mn * (qn - qc) + mc * ms * (qs - qc)

    def diffx(q):
        qc, qe, qw, qn, qs = near_fn(q)
        return 0.5 * (mc * me * (qe - qc) + mc * mw * (qc - qw))

    def diffy(q):
        qc, qe, qw, qn, qs = near_fn(q)
        return 0.5 * (mc * mn * (qn - qc) + mc * ms * (qc - qs))

    uc = near_fn(u_all)[0]
    vc = near_fn(v_all)[0]
    tc = near_fn(t_all)[0]
    sc = near_fn(s_all)[0]
    tend_u = lapl(u_all) + fcor * vc - diffx(press)
    tend_v = lapl(v_all) - fcor * uc - diffy(press)
    new_t = mc * (tc + 0.1 * (lapl(t_all) - uc * diffx(t_all) - vc * diffy(t_all)))
    new_s = mc * (sc + 0.1 * (lapl(s_all) - uc * diffx(s_all) - vc * diffy(s_all)))
    return uc + 0.1 * tend_u, vc + 0.1 * tend_v, new_t, new_s, tend_u, tend_v, mc


def substep(eta, vel_u, vel_v, depth, force_u, force_v, fcor, near_fn, crop):
    wet = (depth > 0).astype(depth.dtype)
    hc, he, hw, hn, hs = near_fn(depth)
    wc, we, ww, wn, ws = near_fn(wet)
    uc, ue, uw, un, us = near_fn(vel_u)
    vc, ve, vw, vn, vs = near_fn(vel_v)
    flux_e = 0.5 * (hc * uc + he * ue) * wc * we
    flux_w = 0.5 * (hw * uw + hc * uc) * wc * ww
    flux_n = 0.5 * (hc * vc + hn * vn) * wc * wn
    flux_s = 0.5 * (hs * vs + hc * vc) * wc * ws
    eta_mid = wc * (crop(eta) - 0.3 * ((flux_e - flux_w) + (flux_n - flux_s)))
    wet_mid = crop(wet)
    ec, ee, ew, en, es = near_fn(eta_mid)
    mc, me, mw, mn, ms = near_fn(wet_mid)
    grad_x = 0.5 * (mc * me * (ee - ec) + mc * mw * (ec - ew))
    grad_y = 0.5 * (mc * mn * (en - ec) + mc * ms * (ec - es))
    old_u = crop(crop(vel_u))
    old_v = crop(crop(vel_v))
    fc = crop(crop(fcor))
    new_u = mc * (old_u + 0.3 * (-grad_x + fc * old_v + crop(crop(force_u))))
    new_v = mc * (old_v + 0.3 * (-grad_y - fc * old_u + crop(crop(force_v))))
    return crop(eta_mid), new_u, new_v


def reference(ocean_state, barotropic, levels):
    ks = jnp.arange(K).astype(jnp.int32)
    wet3 = (ks[:, None, None] < levels[None, :, :]).astype(jnp.float32)
    yy = jnp.arange(NY).astype(jnp.float32)
    fline = 0.5 * (2.0 * (yy + 0.5) / NY - 1.0)
    ext = jnp.concatenate([ocean_state, wet3[None]], axis=0)
    ustar, vstar, new_t, new_s, tend_u, tend_v, mc = baroclinic(ext, fline, near)
    lev = levels.astype(jnp.float32)
    inverse = 1.0 / jnp.maximum(lev, 1.0)
    force_u = jnp.sum(mc * tend_u, axis=0) * inverse
    force_v = jnp.sum(mc * tend_v, axis=0) * inverse
    depth = lev / K
    fcor = jnp.broadcast_to(fline[None, :], (NX, NY))
    eta, vel_u, vel_v = barotropic[0], barotropic[1], barotropic[2]
    total = jnp.zeros((2, NX, NY), jnp.float32)
    for step in range(NSUB):
        eta, vel_u, vel_v = substep(eta, vel_u, vel_v, depth, force_u, force_v, fcor, near, keep)
        total = total + jnp.stack([vel_u, vel_v])
    mean_vel = total * (1.0 / NSUB)
    col_u = jnp.sum(mc * ustar, axis=0) * inverse
    col_v = jnp.sum(mc * vstar, axis=0) * inverse
    new_u = mc * (ustar - col_u + mean_vel[0])
    new_v = mc * (vstar - col_v + mean_vel[1])
    return jnp.stack([new_u, new_v, new_t, new_s]), jnp.stack([eta, vel_u, vel_v])
```

```python
import functools

import jax
import jax.numpy as jnp
from jax import lax
from jax.experimental import pallas as pl
from jax.experimental.pallas import tpu as pltpu
from jax.sharding import PartitionSpec as P

MESH = pl.DeviceIdType.MESH
NSUB = 16
TX = 32
TY = 128
EAST, WEST, NORTH, SOUTH = 0, 1, 2, 3


def iota(shape, dim):
    return lax.broadcasted_iota(jnp.int32, shape, dim)


def turn(a, shift, axis):
    return pltpu.roll(a, shift % a.shape[axis], axis)


def kernel(
    levels_n,
    ocean_hbm,
    baro_hbm,
    lev_hbm,
    out_ref,
    baro_out,
    oc,
    lev_i,
    flat2d,
    rim_out,
    rim_in,
    row_out,
    row_in,
    col_out,
    col_in,
    force,
    frim_out,
    frim_in,
    local_sem,
    send_sem,
    recv_sem,
):
    kk = levels_n
    gx = lax.axis_index("gx")
    gy = lax.axis_index("gy")
    nx = lax.axis_size("gx")
    ny = lax.axis_size("gy")
    xe = lax.rem(gx + 1, nx)
    xw = lax.rem(gx + nx - 1, nx)
    yn = lax.rem(gy + 1, ny)
    ys = lax.rem(gy + ny - 1, ny)
    around = [(x, y) for y in (yn, ys) for x in (xw, gx, xe)]
    everyone = around + [(xw, gy), (xe, gy)]

    barrier = pltpu.get_barrier_semaphore()
    for dev in everyone:
        pl.semaphore_signal(barrier, inc=1, device_id=dev, device_id_type=MESH)

    load_o = pltpu.make_async_copy(ocean_hbm, oc, local_sem.at[0])
    load_b = pltpu.make_async_copy(baro_hbm, flat2d.at[pl.ds(0, 3), pl.ds(TX, TX), :], local_sem.at[1])
    load_l = pltpu.make_async_copy(lev_hbm, lev_i, local_sem.at[2])
    load_o.start()
    load_b.start()
    load_l.start()

    lane = iota((TX, TY), 1)
    row = iota((TX, TY), 0)

    def send(src, dst, index, dev):
        copy = pltpu.make_async_remote_copy(
            src_ref=src,
            dst_ref=dst,
            send_sem=send_sem.at[index],
            recv_sem=recv_sem.at[index],
            device_id=dev,
            device_id_type=MESH,
        )
        copy.start()
        return copy

    load_l.wait()
    lev = lev_i[...].astype(jnp.float32)
    flat2d[3, pl.ds(TX, TX), :] = lev
    load_b.wait()
    quad = [flat2d[f, pl.ds(TX, TX), :] for f in range(4)]
    north = quad[3]
    south = quad[0]
    for f in range(4):
        if f != 3:
            north = jnp.where(lane // 32 == f, turn(quad[f], 32 * (f + 1), 1), north)
        if f != 0:
            south = jnp.where(lane // 32 == f, turn(quad[f], 32 * f, 1), south)
    rim_out[0] = north
    rim_out[1] = south

    load_o.wait()
    row_out[EAST] = oc[pl.ds(0, 4 * kk, stride=TX), :]
    row_out[WEST] = oc[pl.ds(TX - 1, 4 * kk, stride=TX), :]

    step = 8

    def gather_columns(o, carry):
        first, last = carry
        for j in range(step):
            i = o * step + j
            moved = pltpu.roll(oc[pl.ds(pl.multiple_of(i * TX, TX), TX), :], i, 1)
            first = jnp.where(lane == i, moved, first)
            last = jnp.where(lane == lax.rem(i + TY - 1, TY), moved, last)
        return first, last

    zero = jnp.zeros((TX, TY), jnp.float32)
    first, last = lax.fori_loop(0, 4 * kk // step, gather_columns, (zero, zero))
    col_out[0] = first
    col_out[1] = last

    pl.semaphore_wait(barrier, len(everyone))
    copies = [
        send(col_out.at[0], col_in.at[0], 0, (gx, ys)),
        send(col_out.at[1], col_in.at[1], 1, (gx, yn)),
        send(row_out.at[EAST], row_in.at[EAST], 2, (xw, gy)),
        send(row_out.at[WEST], row_in.at[WEST], 3, (xe, gy)),
        send(flat2d.at[:, pl.ds(TX, TX), :], flat2d.at[:, pl.ds(2 * TX, TX), :], 4, (xw, gy)),
        send(flat2d.at[:, pl.ds(TX, TX), :], flat2d.at[:, pl.ds(0, TX), :], 5, (xe, gy)),
    ]
    for s, y in ((0, ys), (1, yn)):
        for j, x in ((0, xe), (1, gx), (2, xw)):
            copies.append(send(rim_out.at[1 - s], rim_in.at[3 * s + j], 6 + 3 * s + j, (x, y)))
    for copy in copies:
        copy.wait()

    top = row == TX - 1
    bottom = row == 0

    def unpack(refs_in, f, start):
        a = turn(refs_in[start], -32 * f, 1)
        b = turn(refs_in[start + 3], 96 - 32 * f, 1)
        return jnp.where(lane < 32, a, jnp.where(lane >= 96, b, 0.0))

    lev_d = unpack(rim_in, 3, 1)
    lev_e = jnp.where(top, flat2d[3, pl.ds(2 * TX, 1), :], turn(lev, -1, 0))
    lev_w = jnp.where(bottom, flat2d[3, pl.ds(TX - 1, 1), :], turn(lev, 1, 0))
    lev_n = jnp.where(lane == TY - 1, turn(lev_d, -1, 1), turn(lev, -1, 1))
    lev_s = jnp.where(lane == 0, turn(lev_d, 1, 1), turn(lev, 1, 1))
    face_e = jnp.minimum(lev, lev_e)
    face_w = jnp.minimum(lev, lev_w)
    face_n = jnp.minimum(lev, lev_n)
    face_s = jnp.minimum(lev, lev_s)
    inverse = 1.0 / jnp.maximum(lev, 1.0)

    row_total = (ny * TY).astype(jnp.float32) if hasattr(ny, "astype") else float(ny * TY)
    y_own = (gy * TY + lane).astype(jnp.float32)
    fcor = 0.5 * (2.0 * (y_own + 0.5) / row_total - 1.0)

    def read(f, k):
        return oc[pl.ds(pl.multiple_of((f * kk + k) * TX, TX), TX), :]

    def rims(f, k):
        i = f * kk + k
        east = row_in[EAST, pl.ds(i, 1), :]
        west = row_in[WEST, pl.ds(i, 1), :]
        back = lax.rem(TY - i, TY)
        return east, west, pltpu.roll(col_in[0], back, 1), pltpu.roll(col_in[1], back, 1)

    def jumps(q, rim, faces):
        east, west, north, south = rim
        qe = jnp.where(top, east, turn(q, -1, 0))
        qw = jnp.where(bottom, west, turn(q, 1, 0))
        qn = turn(jnp.where(lane == 0, north, q), -1, 1)
        qs = turn(jnp.where(lane == TY - 1, south, q), 1, 1)
        return [jnp.where(m, n - q, 0.0) for m, n in zip(faces, (qe, qw, qn, qs))]

    def faces_at(level):
        return [level < m for m in (face_e, face_w, face_n, face_s)]

    def momentum(k, carry):
        press, press_e, press_w, press_n, press_s, sum_u, sum_v, col_u, col_v = carry
        level = k.astype(jnp.float32)
        wet = level < lev
        faces = faces_at(level)
        u = read(0, k)
        v = read(1, k)
        t_rim = rims(2, k)
        s_rim = rims(3, k)

        def add(p, m, s, t):
            return p + jnp.where(m, 0.1 * s - 0.2 * t, 0.0)

        press = add(press, wet, read(3, k), read(2, k))
        press_e = add(press_e, level < edge_e, s_rim[0], t_rim[0])
        press_w = add(press_w, level < edge_w, s_rim[1], t_rim[1])
        press_n = add(press_n, level < lev_d, s_rim[2], t_rim[2])
        press_s = add(press_s, level < lev_d, s_rim[3], t_rim[3])
        pe, pw, pn, ps = jumps(press, (press_e, press_w, press_n, press_s), faces)
        ue, uw, un, us = jumps(u, rims(0, k), faces)
        ve, vw, vn, vs = jumps(v, rims(1, k), faces)
        tend_u = (ue + uw) + (un + us) + fcor * v - 0.5 * (pe - pw)
        tend_v = (ve + vw) + (vn + vs) - fcor * u - 0.5 * (pn - ps)
        star_u = u + 0.1 * tend_u
        star_v = v + 0.1 * tend_v
        out_ref[pl.ds(pl.multiple_of(k * TX, TX), TX), :] = star_u
        out_ref[pl.ds(pl.multiple_of((kk + k) * TX, TX), TX), :] = star_v
        return (
            press,
            press_e,
            press_w,
            press_n,
            press_s,
            sum_u + jnp.where(wet, tend_u, 0.0),
            sum_v + jnp.where(wet, tend_v, 0.0),
            col_u + jnp.where(wet, star_u, 0.0),
            col_v + jnp.where(wet, star_v, 0.0),
        )

    edge_e = flat2d[3, pl.ds(2 * TX, 1), :]
    edge_w = flat2d[3, pl.ds(TX - 1, 1), :]
    line = jnp.zeros((1, TY), jnp.float32)
    sums = lax.fori_loop(0, kk, momentum, (zero, line, line, zero, zero, zero, zero, zero, zero))
    force_u = sums[5] * inverse
    force_v = sums[6] * inverse
    mean_u = sums[7] * inverse
    mean_v = sums[8] * inverse
    force[0, pl.ds(TX, TX), :] = force_u
    force[1, pl.ds(TX, TX), :] = force_v

    half = TX // 2
    lane_h = iota((half, TY), 1)
    parts = [a[h * half : (h + 1) * half] for a in (force_u, force_v) for h in (0, 1)]
    north = parts[3]
    south = parts[0]
    for f in range(4):
        if f != 3:
            north = jnp.where(lane_h // 32 == f, turn(parts[f], 32 * (f + 1), 1), north)
        if f != 0:
            south = jnp.where(lane_h // 32 == f, turn(parts[f], 32 * f, 1), south)
    frim_out[0] = north
    frim_out[1] = south
    copies = []
    for s, y in ((0, ys), (1, yn)):
        for j, x in ((0, xe), (1, gx), (2, xw)):
            copies.append(send(frim_out.at[1 - s], frim_in.at[3 * s + j], 14 + 3 * s + j, (x, y)))
    own = force.at[:, pl.ds(TX, TX), :]
    copies.append(send(own, force.at[:, pl.ds(2 * TX, TX), :], 12, (xw, gy)))
    copies.append(send(own, force.at[:, pl.ds(0, TX), :], 13, (xe, gy)))

    def tracers(k, carry):
        level = k.astype(jnp.float32)
        wet = level < lev
        faces = faces_at(level)
        u = 0.05 * read(0, k)
        v = 0.05 * read(1, k)
        for f in (2, 3):
            q = read(f, k)
            je, jw, jn, js = jumps(q, rims(f, k), faces)
            new = q + (0.1 * ((je + jw) + (jn + js)) - (u * (je - jw) + v * (jn - js)))
            out_ref[pl.ds(pl.multiple_of((f * kk + k) * TX, TX), TX), :] = jnp.where(wet, new, 0.0)
        return carry

    lax.fori_loop(0, kk, tracers, 0)

    state_d = [
        jnp.concatenate([unpack(rim_in, f, j) for j in range(3)], axis=0) for f in range(4)
    ]
    for copy in copies:
        copy.wait()

    def unpack_half(f, start):
        halves = []
        for h in (0, 1):
            at = 32 * (2 * f + h)
            a = turn(frim_in[start], -at, 1)
            b = turn(frim_in[start + 3], 96 - at, 1)
            halves.append(jnp.where(lane_h < 32, a, jnp.where(lane_h >= 96, b, 0.0)))
        return halves

    force_d = [
        jnp.concatenate([h for j in range(3) for h in unpack_half(f, j)], axis=0) for f in range(2)
    ]

    wide = 3 * TX
    lane_w = iota((wide, TY), 1)
    state = [(flat2d[f], state_d[f]) for f in range(4)]
    wet = [(a > 0.0).astype(jnp.float32) for a in state[3]]
    depth = [a * (1.0 / kk) for a in state[3]]

    def east(a):
        return [turn(x, -1, 0) for x in a]

    def west(a):
        return [turn(x, 1, 0) for x in a]

    def meridional(a, shift, at):
        c, d = [turn(x, shift, 1) for x in a]
        edge = iota(c.shape, 1) == at
        return [jnp.where(edge, d, c), jnp.where(edge, c, d)]

    def north_of(a):
        return meridional(a, -1, TY - 1)

    def south_of(a):
        return meridional(a, 1, 0)

    def both(fn, *args):
        return [fn(*pair) for pair in zip(*args)]

    times = lambda a, b: a * b
    coef_e = both(lambda a, b: 0.15 * a * b, wet, east(wet))
    coef_n = both(lambda a, b: 0.15 * a * b, wet, north_of(wet))
    y_d = lax.rem(gy * TY + lane_w + jnp.where(lane_w < TY // 2, TY, -TY) + ny * TY, ny * TY)
    cor = [
        0.15 * (2.0 * ((gy * TY + lane_w).astype(jnp.float32) + 0.5) / row_total - 1.0),
        0.15 * (2.0 * (y_d.astype(jnp.float32) + 0.5) / row_total - 1.0),
    ]
    eta = both(times, wet, state[0])
    vel_u = both(times, wet, state[1])
    vel_v = both(times, wet, state[2])
    push_u = both(lambda w, a: 0.3 * w * a, wet, (force[0], force_d[0]))
    push_v = both(lambda w, a: 0.3 * w * a, wet, (force[1], force_d[1]))
    total_u = zero
    total_v = zero

    per = NSUB // 4
    for group in range(4):
        if group:
            cut = lambda pair: [a[8 : a.shape[0] - 8] for a in pair]
            eta, vel_u, vel_v, push_u, push_v, coef_e, coef_n, cor, depth = [
                cut(a) for a in (eta, vel_u, vel_v, push_u, push_v, coef_e, coef_n, cor, depth)
            ]
        here = TX - 8 * group

        def substep(_, carry):
            eta, vel_u, vel_v, total_u, total_v = carry
            flow_u = both(times, depth, vel_u)
            flow_v = both(times, depth, vel_v)
            flux_e = both(lambda c, a, b: c * (a + b), coef_e, flow_u, east(flow_u))
            flux_n = both(lambda c, a, b: c * (a + b), coef_n, flow_v, north_of(flow_v))
            eta = both(
                lambda h, e, w, n, s: h - ((e - w) + (n - s)),
                eta,
                flux_e,
                west(flux_e),
                flux_n,
                south_of(flux_n),
            )
            grad_e = both(lambda c, a, b: c * (b - a), coef_e, eta, east(eta))
            grad_n = both(lambda c, a, b: c * (b - a), coef_n, eta, north_of(eta))
            new_u = both(
                lambda u, v, f, p, a, b: (u - (a + b)) + (f * v + p),
                vel_u,
                vel_v,
                cor,
                push_u,
                grad_e,
                west(grad_e),
            )
            new_v = both(
                lambda v, u, f, p, a, b: (v - (a + b)) - (f * u - p),
                vel_v,
                vel_u,
                cor,
                push_v,
                grad_n,
                south_of(grad_n),
            )
            total_u = total_u + new_u[0][here : here + TX]
            total_v = total_v + new_v[0][here : here + TX]
            return eta, new_u, new_v, total_u, total_v

        eta, vel_u, vel_v, total_u, total_v = lax.fori_loop(
            0, per, substep, (eta, vel_u, vel_v, total_u, total_v)
        )

    for f, a in enumerate((eta, vel_u, vel_v)):
        baro_out[f] = a[0][8 : 8 + TX]
    shift_u = total_u * (1.0 / NSUB) - mean_u
    shift_v = total_v * (1.0 / NSUB) - mean_v

    def finish(k, carry):
        is_wet = k.astype(jnp.float32) < lev
        for f, shift in ((0, shift_u), (1, shift_v)):
            at = pl.ds(pl.multiple_of((f * kk + k) * TX, TX), TX)
            out_ref[at, :] = jnp.where(is_wet, out_ref[at, :] + shift, 0.0)
        return carry

    lax.fori_loop(0, kk, finish, 0)


def per_device(ocean_state, barotropic, levels):
    kk = ocean_state.shape[1]
    rows = 4 * kk * TX
    f32 = jnp.float32
    new, baro = pl.pallas_call(
        functools.partial(kernel, kk),
        out_shape=(
            jax.ShapeDtypeStruct((rows, TY), f32),
            jax.ShapeDtypeStruct((3, TX, TY), f32),
        ),
        in_specs=[pl.BlockSpec(memory_space=pl.ANY)] * 3,
        out_specs=(
            pl.BlockSpec(memory_space=pltpu.VMEM),
            pl.BlockSpec(memory_space=pltpu.VMEM),
        ),
        scratch_shapes=[
            pltpu.VMEM((rows, TY), f32),
            pltpu.VMEM((TX, TY), jnp.int32),
            pltpu.VMEM((4, 3 * TX, TY), f32),
            pltpu.VMEM((2, TX, TY), f32),
            pltpu.VMEM((6, TX, TY), f32),
            pltpu.VMEM((2, 4 * kk, TY), f32),
            pltpu.VMEM((2, 4 * kk, TY), f32),
            pltpu.VMEM((2, TX, TY), f32),
            pltpu.VMEM((2, TX, TY), f32),
            pltpu.VMEM((2, 3 * TX, TY), f32),
            pltpu.VMEM((2, TX // 2, TY), f32),
            pltpu.VMEM((6, TX // 2, TY), f32),
            pltpu.SemaphoreType.DMA((3,)),
            pltpu.SemaphoreType.DMA((20,)),
            pltpu.SemaphoreType.DMA((20,)),
        ],
        compiler_params=pltpu.CompilerParams(
            collective_id=0, has_side_effects=True, vmem_limit_bytes=32 * 1024 * 1024
        ),
    )(ocean_state.reshape(rows, TY), barotropic, levels)
    return new.reshape(ocean_state.shape), baro


def solution(mesh):
    in_specs = (P(None, None, "gx", "gy"), P(None, "gx", "gy"), P("gx", "gy"))
    out_specs = (P(None, None, "gx", "gy"), P(None, "gx", "gy"))
    return jax.shard_map(
        per_device, mesh=mesh, in_specs=in_specs, out_specs=out_specs, check_vma=False
    )
```

```python
import functools

import jax
import jax.numpy as jnp
from jax import lax
from jax.experimental import pallas as pl
from jax.experimental.pallas import tpu as pltpu
from jax.sharding import PartitionSpec as P

MESH = pl.DeviceIdType.MESH
NSUB = 16
TX = 32
TY = 128
RIM = 32
F32 = jnp.float32


def iota(shape, dim):
    return lax.broadcasted_iota(jnp.int32, shape, dim)


def turn(a, shift, axis):
    return pltpu.roll(a, shift % a.shape[axis], axis)


def at_level(i):
    return pl.ds(pl.multiple_of(i * TX, TX), TX)


def unrolled(n, times, body, carry):
    def several(o, carry):
        for j in range(times):
            carry = body(o * times + j, carry)
        return carry

    return lax.fori_loop(0, n // times, several, carry)


class Link:
    def __init__(self, copy, sends=None, receives=None):
        self.copy, self.sends, self.receives = copy, sends, receives

    def do(self, what, when):
        if when is None:
            what()
        else:
            pl.when(when)(lambda: what())

    def start(self):
        self.do(self.copy.start, self.sends)

    def wait_send(self):
        self.do(self.copy.wait_send, self.sends)

    def wait_recv(self):
        self.do(self.copy.wait_recv, self.receives)


def pack(parts, lane):
    north, south = parts[3], parts[0]
    for f in range(4):
        if f != 3:
            north = jnp.where(lane // RIM == f, turn(parts[f], RIM * (f + 1), 1), north)
        if f != 0:
            south = jnp.where(lane // RIM == f, turn(parts[f], RIM * f, 1), south)
    return north, south


def unpack(north, south, f, lane):
    a = turn(north, -RIM * f, 1)
    b = turn(south, TY - RIM - RIM * f, 1)
    return jnp.where(lane < RIM, a, jnp.where(lane >= TY - RIM, b, 0.0))


def kernel(
    kk,
    ocean_hbm,
    baro_hbm,
    lev_hbm,
    out_ref,
    baro_out,
    shift_out,
    oc,
    press_ref,
    lev_i,
    flat2d,
    rim_out,
    rim_in,
    row_a_out,
    row_a_in,
    row_b_out,
    row_b_in,
    col_a_out,
    col_a_in,
    col_b_out,
    col_b_in,
    force,
    frim_out,
    frim_in,
    local_sem,
    send_sem,
    recv_sem,
):
    gx = lax.axis_index("gx")
    gy = lax.axis_index("gy")
    nx = lax.axis_size("gx")
    ny = lax.axis_size("gy")
    xe = lax.rem(gx + 1, nx)
    xw = lax.rem(gx + nx - 1, nx)
    yn = lax.rem(gy + 1, ny)
    ys = lax.rem(gy + ny - 1, ny)
    has_n = gy < ny - 1
    has_s = gy > 0

    barrier = pltpu.get_barrier_semaphore()

    def greet(x, y):
        pl.semaphore_signal(barrier, inc=1, device_id=(x, y), device_id_type=MESH)

    @pl.when(has_n)
    def _():
        for x in (xw, xe, gx):
            greet(x, yn)

    @pl.when(has_s)
    def _():
        for x in (xw, xe, gx):
            greet(x, ys)

    greet(xw, gy)
    greet(xe, gy)
    greeted = 2 + 3 * (has_n.astype(jnp.int32) + has_s.astype(jnp.int32))

    load_o = pltpu.make_async_copy(ocean_hbm, oc, local_sem.at[0])
    load_b = pltpu.make_async_copy(baro_hbm, flat2d.at[pl.ds(0, 3), pl.ds(TX, TX), :], local_sem.at[1])
    load_l = pltpu.make_async_copy(lev_hbm, lev_i, local_sem.at[2])
    load_l.start()
    load_b.start()
    load_o.start()

    lane = iota((TX, TY), 1)
    row = iota((TX, TY), 0)
    zero = jnp.zeros((TX, TY), F32)
    counter = [0]

    def link(src, dst, dev, sends=None, receives=None):
        index = counter[0]
        counter[0] += 1
        return Link(
            pltpu.make_async_remote_copy(
                src_ref=src,
                dst_ref=dst,
                send_sem=send_sem.at[index],
                recv_sem=recv_sem.at[index],
                device_id=dev,
                device_id_type=MESH,
            ),
            sends,
            receives,
        )

    def southward(src, dst, x=gx):
        return link(src, dst, (x, ys), has_s, has_n)

    def northward(src, dst, x=gx):
        return link(src, dst, (x, yn), has_n, has_s)

    def westward(src, dst):
        return link(src, dst, (xw, gy))

    def eastward(src, dst):
        return link(src, dst, (xe, gy))

    own = pl.ds(TX, TX)
    after = pl.ds(2 * TX, TX)
    before = pl.ds(0, TX)
    links_a = [
        southward(col_a_out.at[0], col_a_in.at[0]),
        northward(col_a_out.at[1], col_a_in.at[1]),
        westward(row_a_out.at[0], row_a_in.at[0]),
        eastward(row_a_out.at[1], row_a_in.at[1]),
    ]
    links_rim = [
        southward(rim_out.at[1], rim_in.at[1]),
        northward(rim_out.at[0], rim_in.at[4]),
    ]
    links_2d = [
        westward(flat2d.at[:, own, :], flat2d.at[:, after, :]),
        eastward(flat2d.at[:, own, :], flat2d.at[:, before, :]),
    ]
    links_b = [
        southward(col_b_out.at[0], col_b_in.at[0]),
        northward(col_b_out.at[1], col_b_in.at[1]),
        westward(row_b_out.at[0], row_b_in.at[0]),
        eastward(row_b_out.at[1], row_b_in.at[1]),
    ]
    links_relay = [
        link(rim_in.at[1], rim_in.at[2], (xw, gy), has_n, has_n),
        link(rim_in.at[1], rim_in.at[0], (xe, gy), has_n, has_n),
        link(rim_in.at[4], rim_in.at[5], (xw, gy), has_s, has_s),
        link(rim_in.at[4], rim_in.at[3], (xe, gy), has_s, has_s),
    ]
    links_force = [
        southward(frim_out.at[1], frim_in.at[0], xe),
        northward(frim_out.at[0], frim_in.at[3], xe),
        southward(frim_out.at[1], frim_in.at[2], xw),
        northward(frim_out.at[0], frim_in.at[5], xw),
        southward(frim_out.at[1], frim_in.at[1]),
        northward(frim_out.at[0], frim_in.at[4]),
        westward(force.at[:, own, :], force.at[:, after, :]),
        eastward(force.at[:, own, :], force.at[:, before, :]),
    ]

    @pl.when(jnp.logical_not(has_n))
    def _():
        rim_in[0:3] = jnp.zeros((3, TX, TY), F32)
        frim_in[0:3] = jnp.zeros((3, TX // 2, TY), F32)

    @pl.when(jnp.logical_not(has_s))
    def _():
        rim_in[3:6] = jnp.zeros((3, TX, TY), F32)
        frim_in[3:6] = jnp.zeros((3, TX // 2, TY), F32)

    load_l.wait()
    lev = lev_i[...].astype(F32)
    flat2d[3, own, :] = lev
    load_b.wait()
    north, south = pack([flat2d[f, own, :] for f in range(4)], lane)
    rim_out[0] = north
    rim_out[1] = south

    load_o.wait()
    for side, x in ((0, 0), (1, TX - 1)):
        row_a_out[side, pl.ds(0, 2 * kk), :] = oc[pl.ds(x, 2 * kk, stride=TX), :]
        row_b_out[side] = oc[pl.ds(2 * kk * TX + x, 2 * kk, stride=TX), :]
        row_a_out[side, pl.ds(3 * kk, 8), :] = jnp.broadcast_to(lev[x : x + 1], (8, TY))

    def gather(k, carry):
        press, first_a, last_a, first_b, last_b = carry
        t = oc[at_level(2 * kk + k), :]
        s = oc[at_level(3 * kk + k), :]
        press = press + jnp.where(k.astype(F32) < lev, 0.1 * s - 0.2 * t, 0.0)
        press_ref[at_level(k), :] = press
        u = oc[at_level(k), :]
        v = oc[at_level(kk + k), :]
        for f, q in ((0, u), (1, v), (2, press)):
            moved = pltpu.roll(q, f * kk + k, 1)
            first_a = jnp.where(lane == f * kk + k, moved, first_a)
            last_a = jnp.where(lane == lax.rem(f * kk + k + TY - 1, TY), moved, last_a)
        for f, q in ((0, t), (1, s)):
            moved = pltpu.roll(q, f * kk + k, 1)
            first_b = jnp.where(lane == f * kk + k, moved, first_b)
            last_b = jnp.where(lane == lax.rem(f * kk + k + TY - 1, TY), moved, last_b)
        return press, first_a, last_a, first_b, last_b

    _, first_a, last_a, first_b, last_b = unrolled(kk, 2, gather, (zero,) * 5)
    last_a = turn(last_a, 1, 1)
    last_b = turn(last_b, 1, 1)
    first_lev = jnp.broadcast_to(lev[:, 0:1], (TX, TY))
    last_lev = jnp.broadcast_to(lev[:, TY - 1 : TY], (TX, TY))
    in_lev = lane >= 96
    col_a_out[0] = jnp.where(in_lev, first_lev, first_a)
    col_a_out[1] = jnp.where(in_lev, last_lev, last_a)
    col_b_out[0] = first_b
    col_b_out[1] = last_b
    for side, x in ((0, 0), (1, TX - 1)):
        row_a_out[side, pl.ds(2 * kk, kk), :] = press_ref[pl.ds(x, kk, stride=TX), :]

    face_e = jnp.where(row == TX - 1, 0.0, jnp.minimum(lev, turn(lev, -1, 0)))
    face_n = jnp.where(lane == TY - 1, 0.0, jnp.minimum(lev, turn(lev, -1, 1)))
    inverse = 1.0 / jnp.maximum(lev, 1.0)
    row_total = float(ny * TY)
    y_own = (gy * TY + lane).astype(F32)
    fcor = 0.5 * (2.0 * (y_own + 0.5) / row_total - 1.0)

    def jumps(q, in_e, in_n):
        e = jnp.where(in_e, turn(q, -1, 0) - q, 0.0)
        n = jnp.where(in_n, turn(q, -1, 1) - q, 0.0)
        return e, turn(e, 1, 0), n, turn(n, 1, 1)

    def momentum(k, carry):
        sum_u, sum_v, col_u, col_v = carry
        level = k.astype(F32)
        wet = level < lev
        in_e = level < face_e
        in_n = level < face_n
        u = oc[at_level(k), :]
        v = oc[at_level(kk + k), :]
        pe, pw, pn, ps = jumps(press_ref[at_level(k), :], in_e, in_n)
        ue, uw, un, us = jumps(u, in_e, in_n)
        ve, vw, vn, vs = jumps(v, in_e, in_n)
        tend_u = ((ue - uw) + (un - us)) + (fcor * v - 0.5 * (pe + pw))
        tend_v = ((ve - vw) + (vn - vs)) - (fcor * u + 0.5 * (pn + ps))
        star_u = u + 0.1 * tend_u
        star_v = v + 0.1 * tend_v
        out_ref[at_level(k), :] = star_u
        out_ref[at_level(kk + k), :] = star_v
        return (
            sum_u + jnp.where(wet, tend_u, 0.0),
            sum_v + jnp.where(wet, tend_v, 0.0),
            col_u + jnp.where(wet, star_u, 0.0),
            col_v + jnp.where(wet, star_v, 0.0),
        )

    def tracers(k, carry):
        level = k.astype(F32)
        wet = level < lev
        in_e = level < face_e
        in_n = level < face_n
        u = 0.05 * oc[at_level(k), :]
        v = 0.05 * oc[at_level(kk + k), :]
        for f in (2, 3):
            q = oc[at_level(f * kk + k), :]
            e, w, n, s = jumps(q, in_e, in_n)
            new = q + (0.1 * ((e - w) + (n - s)) - (u * (e + w) + v * (n + s)))
            out_ref[at_level(f * kk + k), :] = jnp.where(wet, new, 0.0)
        return carry

    sum_u, sum_v, col_u, col_v = unrolled(kk, 2, momentum, (zero,) * 4)

    pl.semaphore_wait(barrier, greeted)
    for x in links_a + links_rim + links_2d + links_b:
        x.start()

    unrolled(kk, 2, tracers, 0)

    for x in links_a:
        x.wait_recv()
    level = iota((kk, TY), 0).astype(F32)
    rows_add = []
    for side, sign in ((0, 1.0), (1, -1.0)):
        mine = row_a_out.at[1 - side]
        theirs = row_a_in.at[side]
        face = jnp.minimum(mine[pl.ds(3 * kk, 1), :], theirs[pl.ds(3 * kk, 1), :])
        wet = level < face
        ju, jv, jp = [
            jnp.where(wet, theirs[pl.ds(f * kk, kk), :] - mine[pl.ds(f * kk, kk), :], 0.0)
            for f in range(3)
        ]
        rows_add.append((wet, ju - (0.5 * sign) * jp, jv))
    cols_add = []
    level_l = jnp.where(lane < kk, lane, jnp.where(lane < 2 * kk, lane - kk, lane - 2 * kk)).astype(F32)
    in_u = lane < kk
    in_v = jnp.logical_and(lane >= kk, lane < 2 * kk)
    in_p = jnp.logical_and(lane >= 2 * kk, lane < 3 * kk)
    for side, sign in ((0, 1.0), (1, -1.0)):
        mine = col_a_out[1 - side]
        theirs = col_a_in[side]
        their_lev = jnp.broadcast_to(theirs[:, TY - 1 : TY], (TX, TY))
        my_lev = last_lev if side == 0 else first_lev
        wet = jnp.logical_and(level_l < jnp.minimum(my_lev, their_lev), (has_n, has_s)[side])
        jump = jnp.where(wet, theirs - mine, 0.0)
        both = jnp.where(in_p, (-0.5 * sign) * jump, jump)
        cols_add.append((wet, both))

    def total(a):
        return jnp.sum(a, axis=0, keepdims=True)

    def across(a, mask):
        return jnp.sum(jnp.where(mask, a, 0.0), axis=1, keepdims=True)

    in_vp = jnp.logical_or(in_v, in_p)
    extra_u = jnp.where(row == TX - 1, total(rows_add[0][1]), 0.0)
    extra_u += jnp.where(row == 0, total(rows_add[1][1]), 0.0)
    extra_u += jnp.where(lane == TY - 1, across(cols_add[0][1], in_u), 0.0)
    extra_u += jnp.where(lane == 0, across(cols_add[1][1], in_u), 0.0)
    extra_v = jnp.where(row == TX - 1, total(rows_add[0][2]), 0.0)
    extra_v += jnp.where(row == 0, total(rows_add[1][2]), 0.0)
    extra_v += jnp.where(lane == TY - 1, across(cols_add[0][1], in_vp), 0.0)
    extra_v += jnp.where(lane == 0, across(cols_add[1][1], in_vp), 0.0)
    force_u = (sum_u + extra_u) * inverse
    force_v = (sum_v + extra_v) * inverse
    force[0, own, :] = force_u
    force[1, own, :] = force_v
    half = TX // 2
    lane_h = iota((half, TY), 1)
    north, south = pack(
        [a[h * half : (h + 1) * half] for a in (force_u, force_v) for h in (0, 1)], lane_h
    )
    frim_out[0] = north
    frim_out[1] = south
    for x in links_force:
        x.start()

    for x in links_rim:
        x.wait_recv()
    for x in links_relay:
        x.start()
    mean_u = (col_u + 0.1 * extra_u) * inverse
    mean_v = (col_v + 0.1 * extra_v) * inverse

    for x in links_b:
        x.wait_recv()
    for side, sign, x in ((0, 1.0, TX - 1), (1, -1.0, 0)):
        wet, add_u, add_v = rows_add[side]
        for f, add in ((0, add_u), (1, add_v)):
            at = pl.ds(f * kk * TX + x, kk, stride=TX)
            out_ref[at, :] = out_ref[at, :] + 0.1 * add
        weight = 0.1 - (0.05 * sign) * row_a_out[1 - side, pl.ds(0, kk), :]
        for f in (0, 1):
            at = pl.ds((2 + f) * kk * TX + x, kk, stride=TX)
            rows = pl.ds(f * kk, kk)
            jump = jnp.where(wet, row_b_in[side, rows, :] - row_b_out[1 - side, rows, :], 0.0)
            out_ref[at, :] = out_ref[at, :] + weight * jump
    patches = []
    for side, sign in ((0, 1.0), (1, -1.0)):
        wet, both = cols_add[side]
        mine = col_a_out[1 - side]
        first = 0.1 * (both + jnp.where(in_v, turn(jnp.where(in_p, both, 0.0), -kk, 1), 0.0))
        v = jnp.where(lane < kk, turn(mine, -kk, 1), mine)
        jump = jnp.where(
            wet,
            col_b_in[side] - col_b_out[1 - side],
            0.0,
        )
        second = (0.1 - (0.05 * sign) * v) * jump
        patch = jnp.where(lane < 2 * kk, first, turn(second, 2 * kk, 1))
        patches.append(patch)
    north, south = turn(patches[0], -1, 1), patches[1]
    odd = lane % 2 == 1
    mixed = [jnp.where(odd, north, south), jnp.where(odd, south, north)]
    outer = jnp.logical_or(lane == 0, lane == TY - 1)

    def patch_columns(o, carry):
        for j in range(4):
            i = o * 4 + j
            add = pltpu.roll(mixed[j % 2], lax.rem(TY - i, TY), 1)
            out_ref[at_level(i), :] = out_ref[at_level(i), :] + jnp.where(outer, add, 0.0)
        return carry

    lax.fori_loop(0, kk, patch_columns, 0)

    for x in links_2d + links_relay:
        x.wait_recv()
    state_d = [
        jnp.concatenate([unpack(rim_in[j], rim_in[3 + j], f, lane) for j in range(3)], axis=0)
        for f in range(4)
    ]
    wide = 3 * TX
    lane_w = iota((wide, TY), 1)
    state = [(flat2d[f], state_d[f]) for f in range(4)]
    wet = [(a > 0.0).astype(F32) for a in state[3]]
    depth = [a * (1.0 / kk) for a in state[3]]

    def east(a):
        return [turn(x, -1, 0) for x in a]

    def west(a):
        return [turn(x, 1, 0) for x in a]

    def meridional(a, shift, at):
        c, d = [turn(x, shift, 1) for x in a]
        edge = iota(c.shape, 1) == at
        return [jnp.where(edge, d, c), jnp.where(edge, c, d)]

    def north_of(a):
        return meridional(a, -1, TY - 1)

    def south_of(a):
        return meridional(a, 1, 0)

    def both(fn, *args):
        return [fn(*pair) for pair in zip(*args)]

    def times(a, b):
        return a * b

    coef_e = both(lambda a, b: 0.15 * a * b, wet, east(wet))
    coef_n = both(lambda a, b: 0.15 * a * b, wet, north_of(wet))
    y_d = lax.rem(gy * TY + lane_w + jnp.where(lane_w < TY // 2, TY, -TY) + ny * TY, ny * TY)
    cor = [
        0.15 * (2.0 * ((gy * TY + lane_w).astype(F32) + 0.5) / row_total - 1.0),
        0.15 * (2.0 * (y_d.astype(F32) + 0.5) / row_total - 1.0),
    ]
    eta = both(times, wet, state[0])
    vel_u = both(times, wet, state[1])
    vel_v = both(times, wet, state[2])

    for x in links_force:
        x.wait_recv()
    force_d = [
        jnp.concatenate(
            [
                unpack(frim_in[j], frim_in[3 + j], 2 * f + h, lane_h)
                for j in range(3)
                for h in (0, 1)
            ],
            axis=0,
        )
        for f in range(2)
    ]
    push_u = both(lambda w, a: 0.3 * w * a, wet, (force[0], force_d[0]))
    push_v = both(lambda w, a: 0.3 * w * a, wet, (force[1], force_d[1]))
    total_u = zero
    total_v = zero

    per = NSUB // 4
    for group in range(4):
        if group:

            def cut(pair):
                return [a[8 : a.shape[0] - 8] for a in pair]

            eta, vel_u, vel_v, push_u, push_v, coef_e, coef_n, cor, depth = [
                cut(a) for a in (eta, vel_u, vel_v, push_u, push_v, coef_e, coef_n, cor, depth)
            ]
        here = TX - 8 * group

        def substep(_, carry):
            eta, vel_u, vel_v, total_u, total_v = carry
            flow_u = both(times, depth, vel_u)
            flow_v = both(times, depth, vel_v)
            flux_e = both(lambda c, a, b: c * (a + b), coef_e, flow_u, east(flow_u))
            flux_n = both(lambda c, a, b: c * (a + b), coef_n, flow_v, north_of(flow_v))
            eta = both(
                lambda h, e, w, n, s: h - ((e - w) + (n - s)),
                eta,
                flux_e,
                west(flux_e),
                flux_n,
                south_of(flux_n),
            )
            grad_e = both(lambda c, a, b: c * (b - a), coef_e, eta, east(eta))
            grad_n = both(lambda c, a, b: c * (b - a), coef_n, eta, north_of(eta))
            new_u = both(
                lambda u, v, f, p, a, b: (u - (a + b)) + (f * v + p),
                vel_u,
                vel_v,
                cor,
                push_u,
                grad_e,
                west(grad_e),
            )
            new_v = both(
                lambda v, u, f, p, a, b: (v - (a + b)) - (f * u - p),
                vel_v,
                vel_u,
                cor,
                push_v,
                grad_n,
                south_of(grad_n),
            )
            total_u = total_u + new_u[0][here : here + TX]
            total_v = total_v + new_v[0][here : here + TX]
            return eta, new_u, new_v, total_u, total_v

        eta, vel_u, vel_v, total_u, total_v = lax.fori_loop(
            0, per, substep, (eta, vel_u, vel_v, total_u, total_v)
        )

    for f, a in enumerate((eta, vel_u, vel_v)):
        baro_out[f] = a[0][8 : 8 + TX]
    shift_out[0] = total_u * (1.0 / NSUB) - mean_u
    shift_out[1] = total_v * (1.0 / NSUB) - mean_v
    shift_out[2] = lev
    for x in links_a + links_rim + links_2d + links_b + links_relay + links_force:
        x.wait_send()


def finish(kk, star, baro, shift, out_hbm, baro_hbm, fast, sems):
    half = 2 * kk * TX
    copies = [
        pltpu.make_async_copy(star.at[pl.ds(half, half), :], out_hbm.at[pl.ds(half, half), :], sems.at[0]),
        pltpu.make_async_copy(baro, baro_hbm, sems.at[1]),
    ]
    for x in copies:
        x.start()
    lev = shift[2]
    for f in (0, 1):
        add = shift[f]

        def body(k, carry):
            i = f * kk + k
            fast[at_level(i), :] = jnp.where(k.astype(F32) < lev, star[at_level(i), :] + add, 0.0)
            return carry

        unrolled(kk, 4, body, 0)
        part = pl.ds(f * kk * TX, kk * TX)
        copies.append(pltpu.make_async_copy(fast.at[part, :], out_hbm.at[part, :], sems.at[2 + f]))
        copies[-1].start()
    for x in copies:
        x.wait()


def per_device(ocean_state, barotropic, levels):
    kk = ocean_state.shape[1]
    rows = 4 * kk * TX
    hbm = pl.BlockSpec(memory_space=pltpu.HBM)
    vmem = pl.BlockSpec(memory_space=pltpu.VMEM)
    links = 24

    def shape(*dims):
        return jax.ShapeDtypeStruct(dims, F32)

    star, baro, shift = pl.pallas_call(
        functools.partial(kernel, kk),
        out_shape=tuple(pltpu.VMEM(d, F32) for d in ((rows, TY), (3, TX, TY), (3, TX, TY))),
        in_specs=[hbm] * 3,
        out_specs=(vmem,) * 3,
        scratch_shapes=[
            pltpu.VMEM((rows, TY), F32),
            pltpu.VMEM((kk * TX, TY), F32),
            pltpu.VMEM((TX, TY), jnp.int32),
            pltpu.VMEM((4, 3 * TX, TY), F32),
            pltpu.VMEM((2, TX, TY), F32),
            pltpu.VMEM((6, TX, TY), F32),
            pltpu.VMEM((2, 3 * kk + 8, TY), F32),
            pltpu.VMEM((2, 3 * kk + 8, TY), F32),
            pltpu.VMEM((2, 2 * kk, TY), F32),
            pltpu.VMEM((2, 2 * kk, TY), F32),
            pltpu.VMEM((2, TX, TY), F32),
            pltpu.VMEM((2, TX, TY), F32),
            pltpu.VMEM((2, TX, TY), F32),
            pltpu.VMEM((2, TX, TY), F32),
            pltpu.VMEM((2, 3 * TX, TY), F32),
            pltpu.VMEM((2, TX // 2, TY), F32),
            pltpu.VMEM((6, TX // 2, TY), F32),
            pltpu.SemaphoreType.DMA((3,)),
            pltpu.SemaphoreType.DMA((links,)),
            pltpu.SemaphoreType.DMA((links,)),
        ],
        compiler_params=pltpu.CompilerParams(
            collective_id=0, has_side_effects=True, vmem_limit_bytes=32 * 1024 * 1024
        ),
        name="ocean_step",
    )(*[pltpu.with_memory_space_constraint(a, pltpu.HBM) for a in (ocean_state.reshape(rows, TY), barotropic, levels)])
    new, baro = pl.pallas_call(
        functools.partial(finish, kk),
        out_shape=(shape(rows, TY), shape(3, TX, TY)),
        in_specs=[vmem] * 3,
        out_specs=(hbm,) * 2,
        scratch_shapes=[
            pltpu.VMEM((2 * kk * TX, TY), F32),
            pltpu.SemaphoreType.DMA((4,)),
        ],
        compiler_params=pltpu.CompilerParams(vmem_limit_bytes=16 * 1024 * 1024),
        name="finish",
    )(star, baro, shift)
    return new.reshape(ocean_state.shape), baro


def solution(mesh):
    in_specs = (P(None, None, "gx", "gy"), P(None, "gx", "gy"), P("gx", "gy"))
    out_specs = (P(None, None, "gx", "gy"), P(None, "gx", "gy"))
    return jax.shard_map(
        per_device, mesh=mesh, in_specs=in_specs, out_specs=out_specs, check_vma=False
    )
```

```python
import functools

import jax
import jax.numpy as jnp
from jax import lax
from jax.experimental import pallas as pl
from jax.experimental.pallas import tpu as pltpu
from jax.sharding import PartitionSpec as P

MESH = pl.DeviceIdType.MESH
NSUB = 16
TX = 32
TY = 128
RIM = 32
MORE = 8
F32 = jnp.float32


def iota(shape, dim):
    return lax.broadcasted_iota(jnp.int32, shape, dim)


def turn(a, shift, axis):
    return pltpu.roll(a, shift % a.shape[axis], axis)


def at_level(i):
    return pl.ds(pl.multiple_of(i * TX, TX), TX)


def unrolled(n, times, body, carry):
    times = min(n, times)

    def several(o, carry):
        for j in range(times):
            carry = body(o * times + j, carry)
        return carry

    return lax.fori_loop(0, n // times, several, carry)


class Link:
    def __init__(self, copy, sends=None, receives=None):
        self.copy, self.sends, self.receives = copy, sends, receives

    def do(self, what, when):
        if when is None:
            what()
        else:
            pl.when(when)(lambda: what())

    def start(self):
        self.do(self.copy.start, self.sends)

    def wait_send(self):
        self.do(self.copy.wait_send, self.sends)

    def wait_recv(self):
        self.do(self.copy.wait_recv, self.receives)


def pack(parts, lane):
    north, south = parts[3], parts[0]
    for f in range(4):
        if f != 3:
            north = jnp.where(lane // RIM == f, turn(parts[f], RIM * (f + 1), 1), north)
        if f != 0:
            south = jnp.where(lane // RIM == f, turn(parts[f], RIM * f, 1), south)
    return north, south


def unpack(north, south, f, lane):
    a = turn(north, -RIM * f, 1)
    b = turn(south, TY - RIM - RIM * f, 1)
    return jnp.where(lane < RIM, a, jnp.where(lane >= TY - RIM, b, 0.0))


def kernel(
    kk,
    ocean_hbm,
    baro_hbm,
    lev_hbm,
    out_ref,
    baro_out,
    shift_out,
    oc,
    press_ref,
    lev_i,
    flat2d,
    rim_out,
    rim_in,
    row_a_out,
    row_a_in,
    row_b_out,
    row_b_in,
    col_a_out,
    col_a_in,
    col_b_out,
    col_b_in,
    force,
    force_d,
    frim_out,
    frim_in,
    eta_ref,
    u_ref,
    v_ref,
    lev_ref,
    coef,
    local_sem,
    send_sem,
    recv_sem,
):
    gx = lax.axis_index("gx")
    gy = lax.axis_index("gy")
    nx = lax.axis_size("gx")
    ny = lax.axis_size("gy")
    xe = lax.rem(gx + 1, nx)
    xw = lax.rem(gx + nx - 1, nx)
    yn = lax.rem(gy + 1, ny)
    ys = lax.rem(gy + ny - 1, ny)
    has_n = gy < ny - 1
    has_s = gy > 0

    barrier = pltpu.get_barrier_semaphore()

    def greet(x, y):
        pl.semaphore_signal(barrier, inc=1, device_id=(x, y), device_id_type=MESH)

    @pl.when(has_n)
    def _():
        for x in (xw, xe, gx):
            greet(x, yn)

    @pl.when(has_s)
    def _():
        for x in (xw, xe, gx):
            greet(x, ys)

    greet(xw, gy)
    greet(xe, gy)
    greeted = 2 + 3 * (has_n.astype(jnp.int32) + has_s.astype(jnp.int32))

    load_o = pltpu.make_async_copy(ocean_hbm, oc, local_sem.at[0])
    load_b = pltpu.make_async_copy(baro_hbm, flat2d.at[pl.ds(0, 3), pl.ds(TX, TX), :], local_sem.at[1])
    load_l = pltpu.make_async_copy(lev_hbm, lev_i, local_sem.at[2])
    load_l.start()
    load_b.start()
    load_o.start()

    lane = iota((TX, TY), 1)
    row = iota((TX, TY), 0)
    zero = jnp.zeros((TX, TY), F32)
    counter = [0]

    def link(src, dst, dev, sends=None, receives=None):
        index = counter[0]
        counter[0] += 1
        return Link(
            pltpu.make_async_remote_copy(
                src_ref=src,
                dst_ref=dst,
                send_sem=send_sem.at[index],
                recv_sem=recv_sem.at[index],
                device_id=dev,
                device_id_type=MESH,
            ),
            sends,
            receives,
        )

    def southward(src, dst, x=gx):
        return link(src, dst, (x, ys), has_s, has_n)

    def northward(src, dst, x=gx):
        return link(src, dst, (x, yn), has_n, has_s)

    def westward(src, dst):
        return link(src, dst, (xw, gy))

    def eastward(src, dst):
        return link(src, dst, (xe, gy))

    own = pl.ds(TX, TX)
    after = pl.ds(2 * TX, TX)
    before = pl.ds(0, TX)
    links_a = [
        southward(col_a_out.at[0], col_a_in.at[0]),
        northward(col_a_out.at[1], col_a_in.at[1]),
        westward(row_a_out.at[0], row_a_in.at[0]),
        eastward(row_a_out.at[1], row_a_in.at[1]),
    ]
    links_rim = [
        southward(rim_out.at[1], rim_in.at[1]),
        northward(rim_out.at[0], rim_in.at[4]),
    ]
    links_2d = [
        westward(flat2d.at[:, own, :], flat2d.at[:, after, :]),
        eastward(flat2d.at[:, own, :], flat2d.at[:, before, :]),
    ]
    links_b = [
        southward(col_b_out.at[0], col_b_in.at[0]),
        northward(col_b_out.at[1], col_b_in.at[1]),
        westward(row_b_out.at[0], row_b_in.at[0]),
        eastward(row_b_out.at[1], row_b_in.at[1]),
    ]
    links_relay = [
        link(rim_in.at[1], rim_in.at[2], (xw, gy), has_n, has_n),
        link(rim_in.at[1], rim_in.at[0], (xe, gy), has_n, has_n),
        link(rim_in.at[4], rim_in.at[5], (xw, gy), has_s, has_s),
        link(rim_in.at[4], rim_in.at[3], (xe, gy), has_s, has_s),
    ]
    links_force = [
        southward(frim_out.at[1], frim_in.at[0], xe),
        northward(frim_out.at[0], frim_in.at[3], xe),
        southward(frim_out.at[1], frim_in.at[2], xw),
        northward(frim_out.at[0], frim_in.at[5], xw),
        southward(frim_out.at[1], frim_in.at[1]),
        northward(frim_out.at[0], frim_in.at[4]),
        westward(force.at[:, own, :], force.at[:, after, :]),
        eastward(force.at[:, own, :], force.at[:, before, :]),
    ]

    @pl.when(jnp.logical_not(has_n))
    def _():
        rim_in[0:3] = jnp.zeros((3, TX, TY), F32)
        frim_in[0:3] = jnp.zeros((3, TX // 2, TY), F32)

    @pl.when(jnp.logical_not(has_s))
    def _():
        rim_in[3:6] = jnp.zeros((3, TX, TY), F32)
        frim_in[3:6] = jnp.zeros((3, TX // 2, TY), F32)

    load_l.wait()
    lev = lev_i[...].astype(F32)
    flat2d[3, own, :] = lev
    load_b.wait()
    north, south = pack([flat2d[f, own, :] for f in range(4)], lane)
    rim_out[0] = north
    rim_out[1] = south

    load_o.wait()
    for side, x in ((0, 0), (1, TX - 1)):
        row_a_out[side, pl.ds(0, 2 * kk), :] = oc[pl.ds(x, 2 * kk, stride=TX), :]
        row_b_out[side] = oc[pl.ds(2 * kk * TX + x, 2 * kk, stride=TX), :]
        row_a_out[side, pl.ds(3 * kk, 8), :] = jnp.broadcast_to(lev[x : x + 1], (8, TY))

    def gather(k, carry):
        press, first_a, last_a, first_b, last_b = carry
        t = oc[at_level(2 * kk + k), :]
        s = oc[at_level(3 * kk + k), :]
        press = press + jnp.where(k.astype(F32) < lev, 0.1 * s - 0.2 * t, 0.0)
        press_ref[at_level(k), :] = press
        u = oc[at_level(k), :]
        v = oc[at_level(kk + k), :]
        for f, q in ((0, u), (1, v), (2, press)):
            moved = pltpu.roll(q, f * kk + k, 1)
            first_a = jnp.where(lane == f * kk + k, moved, first_a)
            last_a = jnp.where(lane == lax.rem(f * kk + k + TY - 1, TY), moved, last_a)
        for f, q in ((0, t), (1, s)):
            moved = pltpu.roll(q, f * kk + k, 1)
            first_b = jnp.where(lane == f * kk + k, moved, first_b)
            last_b = jnp.where(lane == lax.rem(f * kk + k + TY - 1, TY), moved, last_b)
        return press, first_a, last_a, first_b, last_b

    _, first_a, last_a, first_b, last_b = unrolled(kk, MORE, gather, (zero,) * 5)
    last_a = turn(last_a, 1, 1)
    last_b = turn(last_b, 1, 1)
    first_lev = jnp.broadcast_to(lev[:, 0:1], (TX, TY))
    last_lev = jnp.broadcast_to(lev[:, TY - 1 : TY], (TX, TY))
    in_lev = lane >= 96
    col_a_out[0] = jnp.where(in_lev, first_lev, first_a)
    col_a_out[1] = jnp.where(in_lev, last_lev, last_a)
    col_b_out[0] = first_b
    col_b_out[1] = last_b
    for side, x in ((0, 0), (1, TX - 1)):
        row_a_out[side, pl.ds(2 * kk, kk), :] = press_ref[pl.ds(x, kk, stride=TX), :]

    pl.semaphore_wait(barrier, greeted)
    for x in links_a + links_rim + links_2d + links_b:
        x.start()

    face_e = jnp.where(row == TX - 1, 0.0, jnp.minimum(lev, turn(lev, -1, 0)))
    face_n = jnp.where(lane == TY - 1, 0.0, jnp.minimum(lev, turn(lev, -1, 1)))
    inverse = 1.0 / jnp.maximum(lev, 1.0)
    row_total = float(ny * TY)
    y_own = (gy * TY + lane).astype(F32)
    fcor = 0.5 * (2.0 * (y_own + 0.5) / row_total - 1.0)

    def jumps(q, in_e, in_n):
        e = jnp.where(in_e, turn(q, -1, 0) - q, 0.0)
        n = jnp.where(in_n, turn(q, -1, 1) - q, 0.0)
        return e, turn(e, 1, 0), n, turn(n, 1, 1)

    def momentum(k, carry):
        sum_u, sum_v, col_u, col_v = carry
        level = k.astype(F32)
        wet = level < lev
        in_e = level < face_e
        in_n = level < face_n
        u = oc[at_level(k), :]
        v = oc[at_level(kk + k), :]
        pe, pw, pn, ps = jumps(press_ref[at_level(k), :], in_e, in_n)
        ue, uw, un, us = jumps(u, in_e, in_n)
        ve, vw, vn, vs = jumps(v, in_e, in_n)
        tend_u = ((ue - uw) + (un - us)) + (fcor * v - 0.5 * (pe + pw))
        tend_v = ((ve - vw) + (vn - vs)) - (fcor * u + 0.5 * (pn + ps))
        star_u = u + 0.1 * tend_u
        star_v = v + 0.1 * tend_v
        out_ref[at_level(k), :] = star_u
        out_ref[at_level(kk + k), :] = star_v
        return (
            sum_u + jnp.where(wet, tend_u, 0.0),
            sum_v + jnp.where(wet, tend_v, 0.0),
            col_u + jnp.where(wet, star_u, 0.0),
            col_v + jnp.where(wet, star_v, 0.0),
        )

    def tracers(k, carry):
        level = k.astype(F32)
        wet = level < lev
        in_e = level < face_e
        in_n = level < face_n
        u = 0.05 * oc[at_level(k), :]
        v = 0.05 * oc[at_level(kk + k), :]
        for f in (2, 3):
            q = oc[at_level(f * kk + k), :]
            e, w, n, s = jumps(q, in_e, in_n)
            new = q + (0.1 * ((e - w) + (n - s)) - (u * (e + w) + v * (n + s)))
            out_ref[at_level(f * kk + k), :] = jnp.where(wet, new, 0.0)
        return carry

    sum_u, sum_v, col_u, col_v = unrolled(kk, 4, momentum, (zero,) * 4)
    unrolled(kk, MORE, tracers, 0)

    for x in links_a:
        x.wait_recv()
    level = iota((kk, TY), 0).astype(F32)
    rows_add = []
    for side, sign in ((0, 1.0), (1, -1.0)):
        mine = row_a_out.at[1 - side]
        theirs = row_a_in.at[side]
        face = jnp.minimum(mine[pl.ds(3 * kk, 1), :], theirs[pl.ds(3 * kk, 1), :])
        wet = level < face
        ju, jv, jp = [
            jnp.where(wet, theirs[pl.ds(f * kk, kk), :] - mine[pl.ds(f * kk, kk), :], 0.0)
            for f in range(3)
        ]
        rows_add.append((wet, ju - (0.5 * sign) * jp, jv))
    cols_add = []
    level_l = jnp.where(lane < kk, lane, jnp.where(lane < 2 * kk, lane - kk, lane - 2 * kk)).astype(F32)
    in_u = lane < kk
    in_v = jnp.logical_and(lane >= kk, lane < 2 * kk)
    in_p = jnp.logical_and(lane >= 2 * kk, lane < 3 * kk)
    for side, sign in ((0, 1.0), (1, -1.0)):
        mine = col_a_out[1 - side]
        theirs = col_a_in[side]
        their_lev = jnp.broadcast_to(theirs[:, TY - 1 : TY], (TX, TY))
        my_lev = last_lev if side == 0 else first_lev
        wet = jnp.logical_and(level_l < jnp.minimum(my_lev, their_lev), (has_n, has_s)[side])
        jump = jnp.where(wet, theirs - mine, 0.0)
        both = jnp.where(in_p, (-0.5 * sign) * jump, jump)
        cols_add.append((wet, both))

    def total(a):
        return jnp.sum(a, axis=0, keepdims=True)

    def across(a, mask):
        return jnp.sum(jnp.where(mask, a, 0.0), axis=1, keepdims=True)

    in_vp = jnp.logical_or(in_v, in_p)
    extra_u = jnp.where(row == TX - 1, total(rows_add[0][1]), 0.0)
    extra_u += jnp.where(row == 0, total(rows_add[1][1]), 0.0)
    extra_u += jnp.where(lane == TY - 1, across(cols_add[0][1], in_u), 0.0)
    extra_u += jnp.where(lane == 0, across(cols_add[1][1], in_u), 0.0)
    extra_v = jnp.where(row == TX - 1, total(rows_add[0][2]), 0.0)
    extra_v += jnp.where(row == 0, total(rows_add[1][2]), 0.0)
    extra_v += jnp.where(lane == TY - 1, across(cols_add[0][1], in_vp), 0.0)
    extra_v += jnp.where(lane == 0, across(cols_add[1][1], in_vp), 0.0)
    force_u = (sum_u + extra_u) * (0.3 * inverse)
    force_v = (sum_v + extra_v) * (0.3 * inverse)
    force[0, own, :] = force_u
    force[1, own, :] = force_v
    half = TX // 2
    lane_h = iota((half, TY), 1)
    north, south = pack(
        [a[h * half : (h + 1) * half] for a in (force_u, force_v) for h in (0, 1)], lane_h
    )
    frim_out[0] = north
    frim_out[1] = south
    for x in links_force:
        x.start()

    for x in links_rim:
        x.wait_recv()
    for x in links_relay:
        x.start()
    mean_u = (col_u + 0.1 * extra_u) * inverse
    mean_v = (col_v + 0.1 * extra_v) * inverse

    for x in links_b:
        x.wait_recv()
    for side, sign, x in ((0, 1.0, TX - 1), (1, -1.0, 0)):
        wet, add_u, add_v = rows_add[side]
        for f, add in ((0, add_u), (1, add_v)):
            at = pl.ds(f * kk * TX + x, kk, stride=TX)
            out_ref[at, :] = out_ref[at, :] + 0.1 * add
        weight = 0.1 - (0.05 * sign) * row_a_out[1 - side, pl.ds(0, kk), :]
        for f in (0, 1):
            at = pl.ds((2 + f) * kk * TX + x, kk, stride=TX)
            rows = pl.ds(f * kk, kk)
            jump = jnp.where(wet, row_b_in[side, rows, :] - row_b_out[1 - side, rows, :], 0.0)
            out_ref[at, :] = out_ref[at, :] + weight * jump
    patches = []
    for side, sign in ((0, 1.0), (1, -1.0)):
        wet, both = cols_add[side]
        mine = col_a_out[1 - side]
        first = 0.1 * (both + jnp.where(in_v, turn(jnp.where(in_p, both, 0.0), -kk, 1), 0.0))
        v = jnp.where(lane < kk, turn(mine, -kk, 1), mine)
        jump = jnp.where(
            wet,
            col_b_in[side] - col_b_out[1 - side],
            0.0,
        )
        second = (0.1 - (0.05 * sign) * v) * jump
        patch = jnp.where(lane < 2 * kk, first, turn(second, 2 * kk, 1))
        patches.append(patch)
    north, south = turn(patches[0], -1, 1), patches[1]
    odd = lane % 2 == 1
    mixed = [jnp.where(odd, north, south), jnp.where(odd, south, north)]
    outer = jnp.logical_or(lane == 0, lane == TY - 1)

    def patch_columns(i, carry):
        for j in range(2):
            add = pltpu.roll(mixed[j], lax.rem(TY - (2 * i + j), TY), 1)
            at = at_level(2 * i + j)
            out_ref[at, :] = out_ref[at, :] + jnp.where(outer, add, 0.0)
        return carry

    unrolled(2 * kk, 16, patch_columns, 0)

    for x in links_2d + links_relay:
        x.wait_recv()

    def beside(pair, shift):
        c, d = [turn(x, shift, 1) for x in pair]
        edge = iota(c.shape, 1) == (TY - 1 if shift < 0 else 0)
        return jnp.where(edge, d, c), jnp.where(edge, c, d)

    wide = 3 * TX
    edges = jnp.zeros((2, 8, TY), F32)
    for ref in (eta_ref, u_ref, v_ref, lev_ref):
        ref[:, pl.ds(0, 8), :] = edges
        ref[:, pl.ds(8 + wide, 8), :] = edges
    lev_ref[0, pl.ds(8, wide), :] = flat2d[3]
    for j in range(3):
        part = pl.ds(8 + j * TX, TX)
        wet_d = None
        for f, ref in ((3, lev_ref), (0, eta_ref), (1, u_ref), (2, v_ref)):
            q = unpack(rim_in[j], rim_in[3 + j], f, lane)
            if f == 3:
                wet_d = q > 0.0
                wet_c = flat2d[3, pl.ds(j * TX, TX), :] > 0.0
                ref[1, part, :] = q
            else:
                ref[0, part, :] = jnp.where(wet_c, flat2d[f, pl.ds(j * TX, TX), :], 0.0)
                ref[1, part, :] = jnp.where(wet_d, q, 0.0)
    for b in range(0, wide, 8):
        at, ahead, behind = [pl.ds(8 + b + d, 8) for d in (0, 1, -1)]
        here = [lev_ref[h, at, :] for h in range(2)]
        norths = beside(here, -1)
        souths = beside(here, 1)
        for h in range(2):
            is_wet = here[h] > 0.0
            others = (lev_ref[h, ahead, :], lev_ref[h, behind, :], norths[h], souths[h])
            faces = [
                jnp.where(jnp.logical_and(is_wet, other > 0.0), 0.15, 0.0) for other in others
            ]
            scale = 1.0 / kk
            planes = [face * (other * scale) for face, other in zip(faces, others)]
            planes.append((faces[0] - faces[1]) * (here[h] * scale))
            planes.append((faces[2] - faces[3]) * (here[h] * scale))
            for n, plane in enumerate(planes + faces):
                coef[n, h, pl.ds(b, 8), :] = plane

    lane_8 = iota((8, TY), 1)
    y_d = lax.rem(gy * TY + lane_8 + jnp.where(lane_8 < TY // 2, TY, -TY) + ny * TY, ny * TY)
    cor = [
        0.15 * (2.0 * ((gy * TY + lane_8).astype(F32) + 0.5) / row_total - 1.0),
        0.15 * (2.0 * (y_d.astype(F32) + 0.5) / row_total - 1.0),
    ]

    for x in links_force:
        x.wait_recv()
    for j in range(3):
        for f in range(2):
            for h in (0, 1):
                part = pl.ds(j * TX + h * half, half)
                force_d[f, part, :] = unpack(frim_in[j], frim_in[3 + j], 2 * f + h, lane_h)
    push = ((force.at[0], force_d.at[0]), (force.at[1], force_d.at[1]))

    def substep(group, last, totals):
        low, high = 8 * group, wide - 8 * group
        for b in range(low, high, 8):
            at, ahead, behind = [pl.ds(8 + b + d, 8) for d in (0, 1, -1)]
            c_at = pl.ds(b, 8)
            v = [v_ref[h, at, :] for h in range(2)]
            vn = beside(v, -1)
            vs = beside(v, 1)
            for h in range(2):
                c = [coef[n, h, c_at, :] for n in range(6)]
                x = (c[0] * u_ref[h, ahead, :] - c[1] * u_ref[h, behind, :]) + c[4] * u_ref[h, at, :]
                y = (c[2] * vn[h] - c[3] * vs[h]) + c[5] * v[h]
                eta_ref[h, at, :] = eta_ref[h, at, :] - (x + y)
        if last:
            low, high = low + 8, high - 8
        total_u, total_v = [], []
        for b in range(low, high, 8):
            at, ahead, behind = [pl.ds(8 + b + d, 8) for d in (0, 1, -1)]
            c_at = pl.ds(b, 8)
            e = [eta_ref[h, at, :] for h in range(2)]
            en = beside(e, -1)
            es = beside(e, 1)
            for h in range(2):
                c = [coef[n, h, c_at, :] for n in range(6, 10)]
                gx_eta = c[0] * (eta_ref[h, ahead, :] - e[h]) + c[1] * (e[h] - eta_ref[h, behind, :])
                gy_eta = c[2] * (en[h] - e[h]) + c[3] * (e[h] - es[h])
                u = u_ref[h, at, :]
                v = v_ref[h, at, :]
                new_u = (u - gx_eta) + (cor[h] * v + push[0][h][c_at, :])
                new_v = (v - gy_eta) - (cor[h] * u - push[1][h][c_at, :])
                u_ref[h, at, :] = new_u
                v_ref[h, at, :] = new_v
                if h == 0 and TX <= b < 2 * TX:
                    total_u.append(new_u)
                    total_v.append(new_v)
        return (
            totals[0] + jnp.concatenate(total_u, axis=0),
            totals[1] + jnp.concatenate(total_v, axis=0),
        )

    totals = (zero, zero)
    per = NSUB // 4
    for group in range(4):
        for i in range(per):
            totals = substep(group, i == per - 1, totals)
    total_u, total_v = totals

    for f, ref in enumerate((eta_ref, u_ref, v_ref)):
        baro_out[f] = ref[0, pl.ds(8 + TX, TX), :]
    shift_out[0] = total_u * (1.0 / NSUB) - mean_u
    shift_out[1] = total_v * (1.0 / NSUB) - mean_v
    shift_out[2] = lev
    for x in links_a + links_rim + links_2d + links_b + links_relay + links_force:
        x.wait_send()


def finish(kk, star, baro, shift, out_hbm, baro_hbm, fast, sems):
    half = 2 * kk * TX
    copies = [
        pltpu.make_async_copy(star.at[pl.ds(half, half), :], out_hbm.at[pl.ds(half, half), :], sems.at[0]),
        pltpu.make_async_copy(baro, baro_hbm, sems.at[1]),
    ]
    for x in copies:
        x.start()
    lev = shift[2]
    for f in (0, 1):
        add = shift[f]

        def body(k, carry):
            i = f * kk + k
            fast[at_level(i), :] = jnp.where(k.astype(F32) < lev, star[at_level(i), :] + add, 0.0)
            return carry

        unrolled(kk, 4, body, 0)
        part = pl.ds(f * kk * TX, kk * TX)
        copies.append(pltpu.make_async_copy(fast.at[part, :], out_hbm.at[part, :], sems.at[2 + f]))
        copies[-1].start()
    for x in copies:
        x.wait()


def per_device(ocean_state, barotropic, levels):
    kk = ocean_state.shape[1]
    rows = 4 * kk * TX
    hbm = pl.BlockSpec(memory_space=pltpu.HBM)
    vmem = pl.BlockSpec(memory_space=pltpu.VMEM)
    links = 24

    def shape(*dims):
        return jax.ShapeDtypeStruct(dims, F32)

    star, baro, shift = pl.pallas_call(
        functools.partial(kernel, kk),
        out_shape=tuple(pltpu.VMEM(d, F32) for d in ((rows, TY), (3, TX, TY), (3, TX, TY))),
        in_specs=[hbm] * 3,
        out_specs=(vmem,) * 3,
        scratch_shapes=[
            pltpu.VMEM((rows, TY), F32),
            pltpu.VMEM((kk * TX, TY), F32),
            pltpu.VMEM((TX, TY), jnp.int32),
            pltpu.VMEM((4, 3 * TX, TY), F32),
            pltpu.VMEM((2, TX, TY), F32),
            pltpu.VMEM((6, TX, TY), F32),
            pltpu.VMEM((2, 3 * kk + 8, TY), F32),
            pltpu.VMEM((2, 3 * kk + 8, TY), F32),
            pltpu.VMEM((2, 2 * kk, TY), F32),
            pltpu.VMEM((2, 2 * kk, TY), F32),
            pltpu.VMEM((2, TX, TY), F32),
            pltpu.VMEM((2, TX, TY), F32),
            pltpu.VMEM((2, TX, TY), F32),
            pltpu.VMEM((2, TX, TY), F32),
            pltpu.VMEM((2, 3 * TX, TY), F32),
            pltpu.VMEM((2, 3 * TX, TY), F32),
            pltpu.VMEM((2, TX // 2, TY), F32),
            pltpu.VMEM((6, TX // 2, TY), F32),
            pltpu.VMEM((2, 3 * TX + 16, TY), F32),
            pltpu.VMEM((2, 3 * TX + 16, TY), F32),
            pltpu.VMEM((2, 3 * TX + 16, TY), F32),
            pltpu.VMEM((2, 3 * TX + 16, TY), F32),
            pltpu.VMEM((10, 2, 3 * TX, TY), F32),
            pltpu.SemaphoreType.DMA((3,)),
            pltpu.SemaphoreType.DMA((links,)),
            pltpu.SemaphoreType.DMA((links,)),
        ],
        compiler_params=pltpu.CompilerParams(
            collective_id=0, has_side_effects=True, vmem_limit_bytes=32 * 1024 * 1024
        ),
        name="ocean_step",
    )(*[pltpu.with_memory_space_constraint(a, pltpu.HBM) for a in (ocean_state.reshape(rows, TY), barotropic, levels)])
    new, baro = pl.pallas_call(
        functools.partial(finish, kk),
        out_shape=(shape(rows, TY), shape(3, TX, TY)),
        in_specs=[vmem] * 3,
        out_specs=(hbm,) * 2,
        scratch_shapes=[
            pltpu.VMEM((2 * kk * TX, TY), F32),
            pltpu.SemaphoreType.DMA((4,)),
        ],
        compiler_params=pltpu.CompilerParams(vmem_limit_bytes=16 * 1024 * 1024),
        name="finish",
    )(star, baro, shift)
    return new.reshape(ocean_state.shape), baro


def solution(mesh):
    in_specs = (P(None, None, "gx", "gy"), P(None, "gx", "gy"), P("gx", "gy"))
    out_specs = (P(None, None, "gx", "gy"), P(None, "gx", "gy"))
    return jax.shard_map(
        per_device, mesh=mesh, in_specs=in_specs, out_specs=out_specs, check_vma=False
    )
```

```python
import functools

import jax
import jax.numpy as jnp
from jax import lax
from jax.experimental import pallas as pl
from jax.experimental.pallas import tpu as pltpu
from jax.sharding import PartitionSpec as P

MESH = pl.DeviceIdType.MESH
NSUB = 16
TX = 32
TY = 128
RIM = 32
MORE = 8
F32 = jnp.float32


def iota(shape, dim):
    return lax.broadcasted_iota(jnp.int32, shape, dim)


def turn(a, shift, axis):
    return pltpu.roll(a, shift % a.shape[axis], axis)


def at_level(i):
    return pl.ds(pl.multiple_of(i * TX, TX), TX)


def unrolled(n, times, body, carry):
    times = min(n, times)

    def several(o, carry):
        for j in range(times):
            carry = body(o * times + j, carry)
        return carry

    return lax.fori_loop(0, n // times, several, carry)


class Link:
    def __init__(self, copy, sends=None, receives=None):
        self.copy, self.sends, self.receives = copy, sends, receives

    def do(self, what, when):
        if when is None:
            what()
        else:
            pl.when(when)(lambda: what())

    def start(self):
        self.do(self.copy.start, self.sends)

    def wait_send(self):
        self.do(self.copy.wait_send, self.sends)

    def wait_recv(self):
        self.do(self.copy.wait_recv, self.receives)


def pack(parts, lane):
    north, south = parts[3], parts[0]
    for f in range(4):
        if f != 3:
            north = jnp.where(lane // RIM == f, turn(parts[f], RIM * (f + 1), 1), north)
        if f != 0:
            south = jnp.where(lane // RIM == f, turn(parts[f], RIM * f, 1), south)
    return north, south


def unpack(north, south, f, lane):
    a = turn(north, -RIM * f, 1)
    b = turn(south, TY - RIM - RIM * f, 1)
    return jnp.where(lane < RIM, a, jnp.where(lane >= TY - RIM, b, 0.0))


def kernel(
    kk,
    ocean_hbm,
    baro_hbm,
    lev_hbm,
    out_ref,
    baro_out,
    shift_out,
    oc,
    press_ref,
    lev_i,
    flat2d,
    rim_out,
    rim_in,
    row_a_out,
    row_a_in,
    row_b_out,
    row_b_in,
    col_a_out,
    col_a_in,
    col_b_out,
    col_b_in,
    force,
    force_d,
    frim_out,
    frim_in,
    eta_ref,
    u_ref,
    v_ref,
    lev_ref,
    coef,
    local_sem,
    load_sem,
    send_sem,
    recv_sem,
):
    gx = lax.axis_index("gx")
    gy = lax.axis_index("gy")
    nx = lax.axis_size("gx")
    ny = lax.axis_size("gy")
    xe = lax.rem(gx + 1, nx)
    xw = lax.rem(gx + nx - 1, nx)
    yn = lax.rem(gy + 1, ny)
    ys = lax.rem(gy + ny - 1, ny)
    has_n = gy < ny - 1
    has_s = gy > 0

    barrier = pltpu.get_barrier_semaphore()

    def greet(x, y):
        pl.semaphore_signal(barrier, inc=1, device_id=(x, y), device_id_type=MESH)

    @pl.when(has_n)
    def _():
        greet(gx, yn)

    @pl.when(has_s)
    def _():
        greet(gx, ys)

    greet(xw, gy)
    greet(xe, gy)
    greeted = 2 + has_n.astype(jnp.int32) + has_s.astype(jnp.int32)

    some = min(kk, MORE)

    def load(c, f):
        part = pl.ds(pl.multiple_of((f * kk + c * some) * TX, TX), some * TX)
        return pltpu.make_async_copy(ocean_hbm.at[part, :], oc.at[part, :], load_sem.at[c * 4 + f])

    load_b = pltpu.make_async_copy(baro_hbm, flat2d.at[pl.ds(0, 3), pl.ds(TX, TX), :], local_sem.at[1])
    load_l = pltpu.make_async_copy(lev_hbm, lev_i, local_sem.at[2])
    load_l.start()
    load_b.start()
    for c in range(kk // some):
        for f in range(4):
            load(c, f).start()

    lane = iota((TX, TY), 1)
    row = iota((TX, TY), 0)
    zero = jnp.zeros((TX, TY), F32)
    counter = [0]

    def link(src, dst, dev, sends=None, receives=None):
        index = counter[0]
        counter[0] += 1
        return Link(
            pltpu.make_async_remote_copy(
                src_ref=src,
                dst_ref=dst,
                send_sem=send_sem.at[index],
                recv_sem=recv_sem.at[index],
                device_id=dev,
                device_id_type=MESH,
            ),
            sends,
            receives,
        )

    def southward(src, dst, x=gx):
        return link(src, dst, (x, ys), has_s, has_n)

    def northward(src, dst, x=gx):
        return link(src, dst, (x, yn), has_n, has_s)

    def westward(src, dst):
        return link(src, dst, (xw, gy))

    def eastward(src, dst):
        return link(src, dst, (xe, gy))

    own = pl.ds(TX, TX)
    after = pl.ds(2 * TX, TX)
    before = pl.ds(0, TX)
    links_a = [
        southward(col_a_out.at[0], col_a_in.at[0]),
        northward(col_a_out.at[1], col_a_in.at[1]),
        westward(row_a_out.at[0], row_a_in.at[0]),
        eastward(row_a_out.at[1], row_a_in.at[1]),
    ]
    links_rim = [
        southward(rim_out.at[1], rim_in.at[1]),
        northward(rim_out.at[0], rim_in.at[4]),
    ]
    links_2d = [
        westward(flat2d.at[:, own, :], flat2d.at[:, after, :]),
        eastward(flat2d.at[:, own, :], flat2d.at[:, before, :]),
    ]
    links_b = [
        southward(col_b_out.at[0], col_b_in.at[0]),
        northward(col_b_out.at[1], col_b_in.at[1]),
        westward(row_b_out.at[0], row_b_in.at[0]),
        eastward(row_b_out.at[1], row_b_in.at[1]),
    ]
    links_relay = [
        link(rim_in.at[1], rim_in.at[2], (xw, gy), has_n, has_n),
        link(rim_in.at[1], rim_in.at[0], (xe, gy), has_n, has_n),
        link(rim_in.at[4], rim_in.at[5], (xw, gy), has_s, has_s),
        link(rim_in.at[4], rim_in.at[3], (xe, gy), has_s, has_s),
    ]
    links_force = [
        southward(frim_out.at[1], frim_in.at[0], xe),
        northward(frim_out.at[0], frim_in.at[3], xe),
        southward(frim_out.at[1], frim_in.at[2], xw),
        northward(frim_out.at[0], frim_in.at[5], xw),
        southward(frim_out.at[1], frim_in.at[1]),
        northward(frim_out.at[0], frim_in.at[4]),
        westward(force.at[:, own, :], force.at[:, after, :]),
        eastward(force.at[:, own, :], force.at[:, before, :]),
    ]

    @pl.when(jnp.logical_not(has_n))
    def _():
        rim_in[0:3] = jnp.zeros((3, TX, TY), F32)
        frim_in[0:3] = jnp.zeros((3, TX // 2, TY), F32)

    @pl.when(jnp.logical_not(has_s))
    def _():
        rim_in[3:6] = jnp.zeros((3, TX, TY), F32)
        frim_in[3:6] = jnp.zeros((3, TX // 2, TY), F32)

    load_l.wait()
    lev = lev_i[...].astype(F32)
    flat2d[3, own, :] = lev
    load_b.wait()
    north, south = pack([flat2d[f, own, :] for f in range(4)], lane)
    rim_out[0] = north
    rim_out[1] = south

    def gather(k, carry):
        press, first_a, last_a, first_b, last_b = carry
        t = oc[at_level(2 * kk + k), :]
        s = oc[at_level(3 * kk + k), :]
        press = press + jnp.where(k.astype(F32) < lev, 0.1 * s - 0.2 * t, 0.0)
        press_ref[at_level(k), :] = press
        u = oc[at_level(k), :]
        v = oc[at_level(kk + k), :]
        for f, q in ((0, u), (1, v), (2, press)):
            moved = pltpu.roll(q, f * kk + k, 1)
            first_a = jnp.where(lane == f * kk + k, moved, first_a)
            last_a = jnp.where(lane == lax.rem(f * kk + k + TY - 1, TY), moved, last_a)
        for f, q in ((0, t), (1, s)):
            moved = pltpu.roll(q, f * kk + k, 1)
            first_b = jnp.where(lane == f * kk + k, moved, first_b)
            last_b = jnp.where(lane == lax.rem(f * kk + k + TY - 1, TY), moved, last_b)
        return press, first_a, last_a, first_b, last_b

    def gather_chunk(c, carry):
        for f in range(4):
            load(c, f).wait()
        for j in range(some):
            carry = gather(c * some + j, carry)
        return carry

    _, first_a, last_a, first_b, last_b = lax.fori_loop(0, kk // some, gather_chunk, (zero,) * 5)
    last_a = turn(last_a, 1, 1)
    last_b = turn(last_b, 1, 1)
    first_lev = jnp.broadcast_to(lev[:, 0:1], (TX, TY))
    last_lev = jnp.broadcast_to(lev[:, TY - 1 : TY], (TX, TY))
    in_lev = lane >= 96
    col_a_out[0] = jnp.where(in_lev, first_lev, first_a)
    col_a_out[1] = jnp.where(in_lev, last_lev, last_a)
    col_b_out[0] = first_b
    col_b_out[1] = last_b
    for side, x in ((0, 0), (1, TX - 1)):
        row_a_out[side, pl.ds(0, 2 * kk), :] = oc[pl.ds(x, 2 * kk, stride=TX), :]
        row_a_out[side, pl.ds(2 * kk, kk), :] = press_ref[pl.ds(x, kk, stride=TX), :]
        row_a_out[side, pl.ds(3 * kk, 8), :] = jnp.broadcast_to(lev[x : x + 1], (8, TY))
        row_b_out[side] = oc[pl.ds(2 * kk * TX + x, 2 * kk, stride=TX), :]

    pl.semaphore_wait(barrier, greeted)
    for x in links_a + links_rim + links_2d + links_b:
        x.start()

    face_e = jnp.where(row == TX - 1, 0.0, jnp.minimum(lev, turn(lev, -1, 0)))
    face_n = jnp.where(lane == TY - 1, 0.0, jnp.minimum(lev, turn(lev, -1, 1)))
    inverse = 1.0 / jnp.maximum(lev, 1.0)
    row_total = float(ny * TY)
    y_own = (gy * TY + lane).astype(F32)
    fcor = 0.5 * (2.0 * (y_own + 0.5) / row_total - 1.0)

    def jumps(q, in_e, in_n):
        e = jnp.where(in_e, turn(q, -1, 0) - q, 0.0)
        n = jnp.where(in_n, turn(q, -1, 1) - q, 0.0)
        return e, turn(e, 1, 0), n, turn(n, 1, 1)

    def momentum(k, carry):
        sum_u, sum_v, col_u, col_v = carry
        level = k.astype(F32)
        wet = level < lev
        in_e = level < face_e
        in_n = level < face_n
        u = oc[at_level(k), :]
        v = oc[at_level(kk + k), :]
        pe, pw, pn, ps = jumps(press_ref[at_level(k), :], in_e, in_n)
        ue, uw, un, us = jumps(u, in_e, in_n)
        ve, vw, vn, vs = jumps(v, in_e, in_n)
        tend_u = ((ue - uw) + (un - us)) + (fcor * v - 0.5 * (pe + pw))
        tend_v = ((ve - vw) + (vn - vs)) - (fcor * u + 0.5 * (pn + ps))
        star_u = u + 0.1 * tend_u
        star_v = v + 0.1 * tend_v
        out_ref[at_level(k), :] = star_u
        out_ref[at_level(kk + k), :] = star_v
        return (
            sum_u + jnp.where(wet, tend_u, 0.0),
            sum_v + jnp.where(wet, tend_v, 0.0),
            col_u + jnp.where(wet, star_u, 0.0),
            col_v + jnp.where(wet, star_v, 0.0),
        )

    def tracers(k, carry):
        level = k.astype(F32)
        wet = level < lev
        in_e = level < face_e
        in_n = level < face_n
        u = 0.05 * oc[at_level(k), :]
        v = 0.05 * oc[at_level(kk + k), :]
        for f in (2, 3):
            q = oc[at_level(f * kk + k), :]
            e, w, n, s = jumps(q, in_e, in_n)
            new = q + (0.1 * ((e - w) + (n - s)) - (u * (e + w) + v * (n + s)))
            out_ref[at_level(f * kk + k), :] = jnp.where(wet, new, 0.0)
        return carry

    sum_u, sum_v, col_u, col_v = unrolled(kk, 4, momentum, (zero,) * 4)
    unrolled(kk, MORE, tracers, 0)

    for x in links_a:
        x.wait_recv()
    level = iota((kk, TY), 0).astype(F32)
    rows_add = []
    for side, sign in ((0, 1.0), (1, -1.0)):
        mine = row_a_out.at[1 - side]
        theirs = row_a_in.at[side]
        face = jnp.minimum(mine[pl.ds(3 * kk, 1), :], theirs[pl.ds(3 * kk, 1), :])
        wet = level < face
        ju, jv, jp = [
            jnp.where(wet, theirs[pl.ds(f * kk, kk), :] - mine[pl.ds(f * kk, kk), :], 0.0)
            for f in range(3)
        ]
        rows_add.append((wet, ju - (0.5 * sign) * jp, jv))
    cols_add = []
    level_l = jnp.where(lane < kk, lane, jnp.where(lane < 2 * kk, lane - kk, lane - 2 * kk)).astype(F32)
    in_u = lane < kk
    in_v = jnp.logical_and(lane >= kk, lane < 2 * kk)
    in_p = jnp.logical_and(lane >= 2 * kk, lane < 3 * kk)
    for side, sign in ((0, 1.0), (1, -1.0)):
        mine = col_a_out[1 - side]
        theirs = col_a_in[side]
        their_lev = jnp.broadcast_to(theirs[:, TY - 1 : TY], (TX, TY))
        my_lev = last_lev if side == 0 else first_lev
        wet = jnp.logical_and(level_l < jnp.minimum(my_lev, their_lev), (has_n, has_s)[side])
        jump = jnp.where(wet, theirs - mine, 0.0)
        both = jnp.where(in_p, (-0.5 * sign) * jump, jump)
        cols_add.append((wet, both))

    def total(a):
        return jnp.sum(a, axis=0, keepdims=True)

    def across(a, mask):
        return jnp.sum(jnp.where(mask, a, 0.0), axis=1, keepdims=True)

    in_vp = jnp.logical_or(in_v, in_p)
    extra_u = jnp.where(row == TX - 1, total(rows_add[0][1]), 0.0)
    extra_u += jnp.where(row == 0, total(rows_add[1][1]), 0.0)
    extra_u += jnp.where(lane == TY - 1, across(cols_add[0][1], in_u), 0.0)
    extra_u += jnp.where(lane == 0, across(cols_add[1][1], in_u), 0.0)
    extra_v = jnp.where(row == TX - 1, total(rows_add[0][2]), 0.0)
    extra_v += jnp.where(row == 0, total(rows_add[1][2]), 0.0)
    extra_v += jnp.where(lane == TY - 1, across(cols_add[0][1], in_vp), 0.0)
    extra_v += jnp.where(lane == 0, across(cols_add[1][1], in_vp), 0.0)
    force_u = (sum_u + extra_u) * (0.3 * inverse)
    force_v = (sum_v + extra_v) * (0.3 * inverse)
    force[0, own, :] = force_u
    force[1, own, :] = force_v
    half = TX // 2
    lane_h = iota((half, TY), 1)
    north, south = pack(
        [a[h * half : (h + 1) * half] for a in (force_u, force_v) for h in (0, 1)], lane_h
    )
    frim_out[0] = north
    frim_out[1] = south
    for x in links_force:
        x.start()

    for x in links_rim:
        x.wait_recv()
    for x in links_relay:
        x.start()
    mean_u = (col_u + 0.1 * extra_u) * inverse
    mean_v = (col_v + 0.1 * extra_v) * inverse

    for x in links_b:
        x.wait_recv()
    for side, sign, x in ((0, 1.0, TX - 1), (1, -1.0, 0)):
        wet, add_u, add_v = rows_add[side]
        for f, add in ((0, add_u), (1, add_v)):
            at = pl.ds(f * kk * TX + x, kk, stride=TX)
            out_ref[at, :] = out_ref[at, :] + 0.1 * add
        weight = 0.1 - (0.05 * sign) * row_a_out[1 - side, pl.ds(0, kk), :]
        for f in (0, 1):
            at = pl.ds((2 + f) * kk * TX + x, kk, stride=TX)
            rows = pl.ds(f * kk, kk)
            jump = jnp.where(wet, row_b_in[side, rows, :] - row_b_out[1 - side, rows, :], 0.0)
            out_ref[at, :] = out_ref[at, :] + weight * jump
    patches = []
    for side, sign in ((0, 1.0), (1, -1.0)):
        wet, both = cols_add[side]
        mine = col_a_out[1 - side]
        first = 0.1 * (both + jnp.where(in_v, turn(jnp.where(in_p, both, 0.0), -kk, 1), 0.0))
        v = jnp.where(lane < kk, turn(mine, -kk, 1), mine)
        jump = jnp.where(
            wet,
            col_b_in[side] - col_b_out[1 - side],
            0.0,
        )
        second = (0.1 - (0.05 * sign) * v) * jump
        patch = jnp.where(lane < 2 * kk, first, turn(second, 2 * kk, 1))
        patches.append(patch)
    north, south = turn(patches[0], -1, 1), patches[1]
    odd = lane % 2 == 1
    mixed = [jnp.where(odd, north, south), jnp.where(odd, south, north)]
    outer = jnp.logical_or(lane == 0, lane == TY - 1)

    def patch_columns(i, carry):
        for j in range(2):
            add = pltpu.roll(mixed[j], lax.rem(TY - (2 * i + j), TY), 1)
            at = at_level(2 * i + j)
            out_ref[at, :] = out_ref[at, :] + jnp.where(outer, add, 0.0)
        return carry

    unrolled(2 * kk, 16, patch_columns, 0)

    for x in links_2d + links_relay:
        x.wait_recv()

    def beside(pair, shift):
        c, d = [turn(x, shift, 1) for x in pair]
        edge = iota(c.shape, 1) == (TY - 1 if shift < 0 else 0)
        return jnp.where(edge, d, c), jnp.where(edge, c, d)

    wide = 3 * TX
    edges = jnp.zeros((2, 8, TY), F32)
    for ref in (eta_ref, u_ref, v_ref, lev_ref):
        ref[:, pl.ds(0, 8), :] = edges
        ref[:, pl.ds(8 + wide, 8), :] = edges
    lev_ref[0, pl.ds(8, wide), :] = flat2d[3]
    for j in range(3):
        part = pl.ds(8 + j * TX, TX)
        wet_d = None
        for f, ref in ((3, lev_ref), (0, eta_ref), (1, u_ref), (2, v_ref)):
            q = unpack(rim_in[j], rim_in[3 + j], f, lane)
            if f == 3:
                wet_d = q > 0.0
                wet_c = flat2d[3, pl.ds(j * TX, TX), :] > 0.0
                ref[1, part, :] = q
            else:
                ref[0, part, :] = jnp.where(wet_c, flat2d[f, pl.ds(j * TX, TX), :], 0.0)
                ref[1, part, :] = jnp.where(wet_d, q, 0.0)
    for b in range(0, wide, 8):
        at, ahead, behind = [pl.ds(8 + b + d, 8) for d in (0, 1, -1)]
        here = [lev_ref[h, at, :] for h in range(2)]
        norths = beside(here, -1)
        souths = beside(here, 1)
        for h in range(2):
            is_wet = here[h] > 0.0
            others = (lev_ref[h, ahead, :], lev_ref[h, behind, :], norths[h], souths[h])
            faces = [
                jnp.where(jnp.logical_and(is_wet, other > 0.0), 0.15, 0.0) for other in others
            ]
            scale = 1.0 / kk
            planes = [face * (other * scale) for face, other in zip(faces, others)]
            planes.append((faces[0] - faces[1]) * (here[h] * scale))
            planes.append((faces[2] - faces[3]) * (here[h] * scale))
            for n, plane in enumerate(planes + faces):
                coef[n, h, pl.ds(b, 8), :] = plane

    lane_8 = iota((8, TY), 1)
    y_d = lax.rem(gy * TY + lane_8 + jnp.where(lane_8 < TY // 2, TY, -TY) + ny * TY, ny * TY)
    cor = [
        0.15 * (2.0 * ((gy * TY + lane_8).astype(F32) + 0.5) / row_total - 1.0),
        0.15 * (2.0 * (y_d.astype(F32) + 0.5) / row_total - 1.0),
    ]

    push = ((force.at[0], force_d.at[0]), (force.at[1], force_d.at[1]))

    def update_eta(low, high):
        for b in range(low, high, 8):
            at, ahead, behind = [pl.ds(8 + b + d, 8) for d in (0, 1, -1)]
            c_at = pl.ds(b, 8)
            v = [v_ref[h, at, :] for h in range(2)]
            vn = beside(v, -1)
            vs = beside(v, 1)
            for h in range(2):
                c = [coef[n, h, c_at, :] for n in range(6)]
                x = (c[0] * u_ref[h, ahead, :] - c[1] * u_ref[h, behind, :]) + c[4] * u_ref[h, at, :]
                y = (c[2] * vn[h] - c[3] * vs[h]) + c[5] * v[h]
                eta_ref[h, at, :] = eta_ref[h, at, :] - (x + y)

    def update_velocity(low, high, pushed, halves, totals):
        total_u, total_v = [], []
        for b in range(low, high, 8):
            at, ahead, behind = [pl.ds(8 + b + d, 8) for d in (0, 1, -1)]
            c_at = pl.ds(b, 8)
            e = [eta_ref[h, at, :] for h in range(2)]
            en = beside(e, -1)
            es = beside(e, 1)
            for h in range(halves):
                c = [coef[n, h, c_at, :] for n in range(6, 10)]
                gx_eta = c[0] * (eta_ref[h, ahead, :] - e[h]) + c[1] * (e[h] - eta_ref[h, behind, :])
                gy_eta = c[2] * (en[h] - e[h]) + c[3] * (e[h] - es[h])
                u = u_ref[h, at, :]
                v = v_ref[h, at, :]
                add_u = cor[h] * v
                add_v = cor[h] * u
                if pushed:
                    add_u = add_u + push[0][h][c_at, :]
                    add_v = add_v - push[1][h][c_at, :]
                new_u = (u - gx_eta) + add_u
                new_v = (v - gy_eta) - add_v
                u_ref[h, at, :] = new_u
                v_ref[h, at, :] = new_v
                if h == 0 and TX <= b < 2 * TX:
                    total_u.append(new_u)
                    total_v.append(new_v)
        if not pushed:
            return None
        return (
            totals[0] + jnp.concatenate(total_u, axis=0),
            totals[1] + jnp.concatenate(total_v, axis=0),
        )

    update_eta(0, wide)
    update_velocity(0, wide, False, 2, None)
    for x in links_force:
        x.wait_recv()
    for j in range(3):
        for f, ref in ((0, u_ref), (1, v_ref)):
            for h in (0, 1):
                at = j * TX + h * half
                part = pl.ds(at, half)
                inner = pl.ds(8 + at, half)
                add = unpack(frim_in[j], frim_in[3 + j], 2 * f + h, lane_h)
                force_d[f, part, :] = add
                ref[1, inner, :] = ref[1, inner, :] + add
                ref[0, inner, :] = ref[0, inner, :] + force[f, part, :]
    totals = (u_ref[0, pl.ds(8 + TX, TX), :], v_ref[0, pl.ds(8 + TX, TX), :])
    per = NSUB // 4
    for step in range(1, NSUB):
        group, i = step // per, step % per
        low, high = 8 * group, wide - 8 * group
        update_eta(low, high)
        if i == per - 1:
            low, high = low + 8, high - 8
        totals = update_velocity(low, high, True, 1 if step == NSUB - 1 else 2, totals)
    total_u, total_v = totals

    for f, ref in enumerate((eta_ref, u_ref, v_ref)):
        baro_out[f] = ref[0, pl.ds(8 + TX, TX), :]
    shift_out[0] = total_u * (1.0 / NSUB) - mean_u
    shift_out[1] = total_v * (1.0 / NSUB) - mean_v
    shift_out[2] = lev
    for x in links_a + links_rim + links_2d + links_b + links_relay + links_force:
        x.wait_send()


def finish(kk, star, baro, shift, out_hbm, baro_hbm, fast, sems):
    half = 2 * kk * TX
    copies = [
        pltpu.make_async_copy(star.at[pl.ds(half, half), :], out_hbm.at[pl.ds(half, half), :], sems.at[0]),
        pltpu.make_async_copy(baro, baro_hbm, sems.at[1]),
    ]
    for x in copies:
        x.start()
    lev = shift[2]
    for f in (0, 1):
        add = shift[f]

        def body(k, carry):
            i = f * kk + k
            fast[at_level(i), :] = jnp.where(k.astype(F32) < lev, star[at_level(i), :] + add, 0.0)
            return carry

        unrolled(kk, 4, body, 0)
        part = pl.ds(f * kk * TX, kk * TX)
        copies.append(pltpu.make_async_copy(fast.at[part, :], out_hbm.at[part, :], sems.at[2 + f]))
        copies[-1].start()
    for x in copies:
        x.wait()


def per_device(ocean_state, barotropic, levels):
    kk = ocean_state.shape[1]
    rows = 4 * kk * TX
    hbm = pl.BlockSpec(memory_space=pltpu.HBM)
    vmem = pl.BlockSpec(memory_space=pltpu.VMEM)
    links = 24

    def shape(*dims):
        return jax.ShapeDtypeStruct(dims, F32)

    star, baro, shift = pl.pallas_call(
        functools.partial(kernel, kk),
        out_shape=tuple(pltpu.VMEM(d, F32) for d in ((rows, TY), (3, TX, TY), (3, TX, TY))),
        in_specs=[hbm] * 3,
        out_specs=(vmem,) * 3,
        scratch_shapes=[
            pltpu.VMEM((rows, TY), F32),
            pltpu.VMEM((kk * TX, TY), F32),
            pltpu.VMEM((TX, TY), jnp.int32),
            pltpu.VMEM((4, 3 * TX, TY), F32),
            pltpu.VMEM((2, TX, TY), F32),
            pltpu.VMEM((6, TX, TY), F32),
            pltpu.VMEM((2, 3 * kk + 8, TY), F32),
            pltpu.VMEM((2, 3 * kk + 8, TY), F32),
            pltpu.VMEM((2, 2 * kk, TY), F32),
            pltpu.VMEM((2, 2 * kk, TY), F32),
            pltpu.VMEM((2, TX, TY), F32),
            pltpu.VMEM((2, TX, TY), F32),
            pltpu.VMEM((2, TX, TY), F32),
            pltpu.VMEM((2, TX, TY), F32),
            pltpu.VMEM((2, 3 * TX, TY), F32),
            pltpu.VMEM((2, 3 * TX, TY), F32),
            pltpu.VMEM((2, TX // 2, TY), F32),
            pltpu.VMEM((6, TX // 2, TY), F32),
            pltpu.VMEM((2, 3 * TX + 16, TY), F32),
            pltpu.VMEM((2, 3 * TX + 16, TY), F32),
            pltpu.VMEM((2, 3 * TX + 16, TY), F32),
            pltpu.VMEM((2, 3 * TX + 16, TY), F32),
            pltpu.VMEM((10, 2, 3 * TX, TY), F32),
            pltpu.SemaphoreType.DMA((3,)),
            pltpu.SemaphoreType.DMA((4 * max(1, kk // MORE),)),
            pltpu.SemaphoreType.DMA((links,)),
            pltpu.SemaphoreType.DMA((links,)),
        ],
        compiler_params=pltpu.CompilerParams(
            collective_id=0, has_side_effects=True, vmem_limit_bytes=32 * 1024 * 1024
        ),
        name="ocean_step",
    )(*[pltpu.with_memory_space_constraint(a, pltpu.HBM) for a in (ocean_state.reshape(rows, TY), barotropic, levels)])
    new, baro = pl.pallas_call(
        functools.partial(finish, kk),
        out_shape=(shape(rows, TY), shape(3, TX, TY)),
        in_specs=[vmem] * 3,
        out_specs=(hbm,) * 2,
        scratch_shapes=[
            pltpu.VMEM((2 * kk * TX, TY), F32),
            pltpu.SemaphoreType.DMA((4,)),
        ],
        compiler_params=pltpu.CompilerParams(vmem_limit_bytes=16 * 1024 * 1024),
        name="finish",
    )(star, baro, shift)
    return new.reshape(ocean_state.shape), baro


def solution(mesh):
    in_specs = (P(None, None, "gx", "gy"), P(None, "gx", "gy"), P("gx", "gy"))
    out_specs = (P(None, None, "gx", "gy"), P(None, "gx", "gy"))
    return jax.shard_map(
        per_device, mesh=mesh, in_specs=in_specs, out_specs=out_specs, check_vma=False
    )
```

```python
import functools

import jax
import jax.numpy as jnp
from jax import lax
from jax.experimental import pallas as pl
from jax.experimental.pallas import tpu as pltpu
from jax.sharding import PartitionSpec as P

MESH = pl.DeviceIdType.MESH
NSUB = 16
TX = 32
TY = 128
RIM = 32
MORE = 8
F32 = jnp.float32


def iota(shape, dim):
    return lax.broadcasted_iota(jnp.int32, shape, dim)


def turn(a, shift, axis):
    return pltpu.roll(a, shift % a.shape[axis], axis)


def at_level(i):
    return pl.ds(pl.multiple_of(i * TX, TX), TX)


def unrolled(n, times, body, carry):
    times = min(n, times)

    def several(o, carry):
        for j in range(times):
            carry = body(o * times + j, carry)
        return carry

    return lax.fori_loop(0, n // times, several, carry)


class Link:
    def __init__(self, copy, sends=None, receives=None):
        self.copy, self.sends, self.receives = copy, sends, receives

    def do(self, what, when):
        if when is None:
            what()
        else:
            pl.when(when)(lambda: what())

    def start(self):
        self.do(self.copy.start, self.sends)

    def wait_send(self):
        self.do(self.copy.wait_send, self.sends)

    def wait_recv(self):
        self.do(self.copy.wait_recv, self.receives)


def pack(parts, lane):
    north, south = parts[3], parts[0]
    for f in range(4):
        if f != 3:
            north = jnp.where(lane // RIM == f, turn(parts[f], RIM * (f + 1), 1), north)
        if f != 0:
            south = jnp.where(lane // RIM == f, turn(parts[f], RIM * f, 1), south)
    return north, south


def unpack(north, south, f, lane):
    a = turn(north, -RIM * f, 1)
    b = turn(south, TY - RIM - RIM * f, 1)
    return jnp.where(lane < RIM, a, jnp.where(lane >= TY - RIM, b, 0.0))


def kernel(
    kk,
    ocean_hbm,
    baro_hbm,
    lev_hbm,
    out_ref,
    baro_out,
    shift_out,
    oc,
    press_ref,
    lev_i,
    flat2d,
    rim_out,
    rim_in,
    row_a_out,
    row_a_in,
    row_b_out,
    row_b_in,
    cols_in,
    col_b_out,
    col_b_in,
    force,
    push,
    frim_out,
    frim_in,
    eta_ref,
    u_ref,
    v_ref,
    lev_ref,
    coef,
    local_sem,
    load_sem,
    send_sem,
    recv_sem,
):
    gx = lax.axis_index("gx")
    gy = lax.axis_index("gy")
    nx = lax.axis_size("gx")
    ny = lax.axis_size("gy")
    xe = lax.rem(gx + 1, nx)
    xw = lax.rem(gx + nx - 1, nx)
    yn = lax.rem(gy + 1, ny)
    ys = lax.rem(gy + ny - 1, ny)
    has_n = gy < ny - 1
    has_s = gy > 0

    barrier = pltpu.get_barrier_semaphore()

    def greet(x, y):
        pl.semaphore_signal(barrier, inc=1, device_id=(x, y), device_id_type=MESH)

    @pl.when(has_n)
    def _():
        greet(gx, yn)

    @pl.when(has_s)
    def _():
        greet(gx, ys)

    greet(xw, gy)
    greet(xe, gy)
    greeted = 2 + has_n.astype(jnp.int32) + has_s.astype(jnp.int32)

    some = min(kk, MORE)

    def load(c, f):
        part = pl.ds(pl.multiple_of((f * kk + c * some) * TX, TX), some * TX)
        return pltpu.make_async_copy(ocean_hbm.at[part, :], oc.at[part, :], load_sem.at[c * 4 + f])

    load_b = pltpu.make_async_copy(baro_hbm, flat2d.at[pl.ds(0, 3), pl.ds(TX, TX), :], local_sem.at[1])
    load_l = pltpu.make_async_copy(lev_hbm, lev_i, local_sem.at[2])
    load_l.start()
    load_b.start()
    for c in range(kk // some):
        for f in range(4):
            load(c, f).start()

    lane = iota((TX, TY), 1)
    row = iota((TX, TY), 0)
    zero = jnp.zeros((TX, TY), F32)
    counter = [0]

    def link(src, dst, dev, sends=None, receives=None):
        index = counter[0]
        counter[0] += 1
        return Link(
            pltpu.make_async_remote_copy(
                src_ref=src,
                dst_ref=dst,
                send_sem=send_sem.at[index],
                recv_sem=recv_sem.at[index],
                device_id=dev,
                device_id_type=MESH,
            ),
            sends,
            receives,
        )

    def southward(src, dst, x=gx):
        return link(src, dst, (x, ys), has_s, has_n)

    def northward(src, dst, x=gx):
        return link(src, dst, (x, yn), has_n, has_s)

    def westward(src, dst):
        return link(src, dst, (xw, gy))

    def eastward(src, dst):
        return link(src, dst, (xe, gy))

    own = pl.ds(TX, TX)
    after = pl.ds(2 * TX, TX)
    before = pl.ds(0, TX)
    links_a = [
        westward(row_a_out.at[0], row_a_in.at[0]),
        eastward(row_a_out.at[1], row_a_in.at[1]),
    ]
    links_rim = [
        southward(rim_out.at[1], rim_in.at[1]),
        northward(rim_out.at[0], rim_in.at[4]),
    ]
    columns = rim_out.at[:, pl.ds(TX, TX), :]
    links_2d = [
        westward(columns, cols_in.at[1]),
        eastward(columns, cols_in.at[0]),
        westward(flat2d.at[:, own, :], flat2d.at[:, after, :]),
        eastward(flat2d.at[:, own, :], flat2d.at[:, before, :]),
    ]
    links_b = [
        southward(col_b_out.at[0], col_b_in.at[0]),
        northward(col_b_out.at[1], col_b_in.at[1]),
        westward(row_b_out.at[0], row_b_in.at[0]),
        eastward(row_b_out.at[1], row_b_in.at[1]),
    ]
    links_relay = [
        link(rim_in.at[1], rim_in.at[2], (xw, gy), has_n, has_n),
        link(rim_in.at[1], rim_in.at[0], (xe, gy), has_n, has_n),
        link(rim_in.at[4], rim_in.at[5], (xw, gy), has_s, has_s),
        link(rim_in.at[4], rim_in.at[3], (xe, gy), has_s, has_s),
    ]
    links_force = [
        southward(frim_out.at[1], frim_in.at[0], xe),
        northward(frim_out.at[0], frim_in.at[3], xe),
        southward(frim_out.at[1], frim_in.at[2], xw),
        northward(frim_out.at[0], frim_in.at[5], xw),
        southward(frim_out.at[1], frim_in.at[1]),
        northward(frim_out.at[0], frim_in.at[4]),
        westward(force.at[:, own, :], force.at[:, after, :]),
        eastward(force.at[:, own, :], force.at[:, before, :]),
    ]

    @pl.when(jnp.logical_not(has_n))
    def _():
        rim_in[0:3] = jnp.zeros((3, 2 * TX, TY), F32)
        frim_in[0:3] = jnp.zeros((3, TX // 2, TY), F32)

    @pl.when(jnp.logical_not(has_s))
    def _():
        rim_in[3:6] = jnp.zeros((3, 2 * TX, TY), F32)
        frim_in[3:6] = jnp.zeros((3, TX // 2, TY), F32)

    load_l.wait()
    lev = lev_i[...].astype(F32)
    flat2d[3, own, :] = lev
    load_b.wait()
    north, south = pack([flat2d[f, own, :] for f in range(4)], lane)
    rim_out[0, pl.ds(0, TX), :] = north
    rim_out[1, pl.ds(0, TX), :] = south

    def gather(k, carry):
        press, first_a, last_a, first_b, last_b = carry
        t = oc[at_level(2 * kk + k), :]
        s = oc[at_level(3 * kk + k), :]
        press = press + jnp.where(k.astype(F32) < lev, 0.1 * s - 0.2 * t, 0.0)
        press_ref[at_level(k), :] = press
        u = oc[at_level(k), :]
        v = oc[at_level(kk + k), :]
        for f, q in ((0, u), (1, v), (2, press)):
            moved = pltpu.roll(q, f * kk + k, 1)
            first_a = jnp.where(lane == f * kk + k, moved, first_a)
            last_a = jnp.where(lane == lax.rem(f * kk + k + TY - 1, TY), moved, last_a)
        for f, q in ((0, t), (1, s)):
            moved = pltpu.roll(q, f * kk + k, 1)
            first_b = jnp.where(lane == f * kk + k, moved, first_b)
            last_b = jnp.where(lane == lax.rem(f * kk + k + TY - 1, TY), moved, last_b)
        return press, first_a, last_a, first_b, last_b

    def gather_chunk(c, carry):
        for f in range(4):
            load(c, f).wait()
        for j in range(some):
            carry = gather(c * some + j, carry)
        return carry

    _, first_a, last_a, first_b, last_b = lax.fori_loop(0, kk // some, gather_chunk, (zero,) * 5)
    last_a = turn(last_a, 1, 1)
    last_b = turn(last_b, 1, 1)
    first_lev = jnp.broadcast_to(lev[:, 0:1], (TX, TY))
    last_lev = jnp.broadcast_to(lev[:, TY - 1 : TY], (TX, TY))
    in_lev = lane >= 96
    rim_out[0, pl.ds(TX, TX), :] = jnp.where(in_lev, last_lev, last_a)
    rim_out[1, pl.ds(TX, TX), :] = jnp.where(in_lev, first_lev, first_a)
    col_b_out[0] = first_b
    col_b_out[1] = last_b
    for side, x in ((0, 0), (1, TX - 1)):
        row_a_out[side, pl.ds(0, 2 * kk), :] = oc[pl.ds(x, 2 * kk, stride=TX), :]
        row_a_out[side, pl.ds(2 * kk, kk), :] = press_ref[pl.ds(x, kk, stride=TX), :]
        row_a_out[side, pl.ds(3 * kk, 8), :] = jnp.broadcast_to(lev[x : x + 1], (8, TY))
        row_b_out[side] = oc[pl.ds(2 * kk * TX + x, 2 * kk, stride=TX), :]

    pl.semaphore_wait(barrier, greeted)
    for x in links_a + links_rim + links_2d + links_b:
        x.start()

    face_e = jnp.where(row == TX - 1, 0.0, jnp.minimum(lev, turn(lev, -1, 0)))
    face_n = jnp.where(lane == TY - 1, 0.0, jnp.minimum(lev, turn(lev, -1, 1)))
    inverse = 1.0 / jnp.maximum(lev, 1.0)
    row_total = float(ny * TY)
    y_own = (gy * TY + lane).astype(F32)
    fcor = 0.5 * (2.0 * (y_own + 0.5) / row_total - 1.0)

    def jumps(q, in_e, in_n):
        e = jnp.where(in_e, turn(q, -1, 0) - q, 0.0)
        n = jnp.where(in_n, turn(q, -1, 1) - q, 0.0)
        return e, turn(e, 1, 0), n, turn(n, 1, 1)

    def momentum(k, carry):
        sum_u, sum_v, col_u, col_v = carry
        level = k.astype(F32)
        wet = level < lev
        in_e = level < face_e
        in_n = level < face_n
        u = oc[at_level(k), :]
        v = oc[at_level(kk + k), :]
        pe, pw, pn, ps = jumps(press_ref[at_level(k), :], in_e, in_n)
        ue, uw, un, us = jumps(u, in_e, in_n)
        ve, vw, vn, vs = jumps(v, in_e, in_n)
        tend_u = ((ue - uw) + (un - us)) + (fcor * v - 0.5 * (pe + pw))
        tend_v = ((ve - vw) + (vn - vs)) - (fcor * u + 0.5 * (pn + ps))
        star_u = u + 0.1 * tend_u
        star_v = v + 0.1 * tend_v
        out_ref[at_level(k), :] = star_u
        out_ref[at_level(kk + k), :] = star_v
        return (
            sum_u + jnp.where(wet, tend_u, 0.0),
            sum_v + jnp.where(wet, tend_v, 0.0),
            col_u + jnp.where(wet, star_u, 0.0),
            col_v + jnp.where(wet, star_v, 0.0),
        )

    def tracers(k, carry):
        level = k.astype(F32)
        wet = level < lev
        in_e = level < face_e
        in_n = level < face_n
        u = 0.05 * oc[at_level(k), :]
        v = 0.05 * oc[at_level(kk + k), :]
        for f in (2, 3):
            q = oc[at_level(f * kk + k), :]
            e, w, n, s = jumps(q, in_e, in_n)
            new = q + (0.1 * ((e - w) + (n - s)) - (u * (e + w) + v * (n + s)))
            out_ref[at_level(f * kk + k), :] = jnp.where(wet, new, 0.0)
        return carry

    sum_u, sum_v, col_u, col_v = unrolled(kk, 4, momentum, (zero,) * 4)
    unrolled(kk, MORE, tracers, 0)

    for x in links_a:
        x.wait_recv()
    level = iota((kk, TY), 0).astype(F32)
    rows_add = []
    for side, sign in ((0, 1.0), (1, -1.0)):
        mine = row_a_out.at[1 - side]
        theirs = row_a_in.at[side]
        face = jnp.minimum(mine[pl.ds(3 * kk, 1), :], theirs[pl.ds(3 * kk, 1), :])
        wet = level < face
        ju, jv, jp = [
            jnp.where(wet, theirs[pl.ds(f * kk, kk), :] - mine[pl.ds(f * kk, kk), :], 0.0)
            for f in range(3)
        ]
        rows_add.append((wet, ju - (0.5 * sign) * jp, jv))

    def total(a):
        return jnp.sum(a, axis=0, keepdims=True)

    zonal_u = jnp.where(row == TX - 1, total(rows_add[0][1]), 0.0)
    zonal_u += jnp.where(row == 0, total(rows_add[1][1]), 0.0)
    zonal_v = jnp.where(row == TX - 1, total(rows_add[0][2]), 0.0)
    zonal_v += jnp.where(row == 0, total(rows_add[1][2]), 0.0)
    force_u = (sum_u + zonal_u) * (0.3 * inverse)
    force_v = (sum_v + zonal_v) * (0.3 * inverse)
    force[0, own, :] = force_u
    force[1, own, :] = force_v
    half = TX // 2
    lane_h = iota((half, TY), 1)
    north, south = pack(
        [a[h * half : (h + 1) * half] for a in (force_u, force_v) for h in (0, 1)], lane_h
    )
    frim_out[0] = north
    frim_out[1] = south
    for x in links_force:
        x.start()

    for x in links_rim:
        x.wait_recv()
    for x in links_relay:
        x.start()

    level_l = jnp.where(lane < kk, lane, jnp.where(lane < 2 * kk, lane - kk, lane - 2 * kk)).astype(F32)
    in_u = lane < kk
    in_v = jnp.logical_and(lane >= kk, lane < 2 * kk)
    in_p = jnp.logical_and(lane >= 2 * kk, lane < 3 * kk)

    def across(a, mask):
        return jnp.sum(jnp.where(mask, a, 0.0), axis=1, keepdims=True)

    def meridional_face(side, mine, theirs):
        sign = (1.0, -1.0)[side]
        near, far = (TY - 1, 0) if side == 0 else (0, TY - 1)
        my_lev, their_lev = [jnp.broadcast_to(a[:, TY - 1 : TY], (TX, TY)) for a in (mine, theirs)]
        wet = level_l < jnp.minimum(my_lev, their_lev)
        jump = jnp.where(wet, theirs - mine, 0.0)
        jump_u = across(jump, in_u)
        jump_v = across(jump, in_v)
        jump_p = (0.5 * sign) * across(jump, in_p)
        here = [jnp.where(lane == near, a, 0.0) for a in (jump_u, jump_v - jump_p)]
        there = [jnp.where(lane == far, a, 0.0) for a in (-jump_u, -jump_v - jump_p)]
        scale = [0.3 / jnp.maximum(a, 1.0) for a in (my_lev, their_lev)]
        return wet, jump, here, [a * scale[0] for a in here], [a * scale[1] for a in there]

    def meridional_faces(j, mine):
        faces = [
            meridional_face(side, mine[side], rim_in[3 * side + j, pl.ds(TX, TX), :])
            for side in range(2)
        ]
        for f in range(2):
            push[f, 0, pl.ds(j * TX, TX), :] = faces[0][3][f] + faces[1][3][f]
            push[f, 1, pl.ds(j * TX, TX), :] = faces[0][4][f] + faces[1][4][f]
        return faces

    my_columns = [rim_out[side, pl.ds(TX, TX), :] for side in range(2)]
    faces = meridional_faces(1, my_columns)
    mean_u = (col_u + 0.1 * (zonal_u + faces[0][2][0] + faces[1][2][0])) * inverse
    mean_v = (col_v + 0.1 * (zonal_v + faces[0][2][1] + faces[1][2][1])) * inverse

    for x in links_b:
        x.wait_recv()
    for side, sign, x in ((0, 1.0, TX - 1), (1, -1.0, 0)):
        wet, add_u, add_v = rows_add[side]
        for f, add in ((0, add_u), (1, add_v)):
            at = pl.ds(f * kk * TX + x, kk, stride=TX)
            out_ref[at, :] = out_ref[at, :] + 0.1 * add
        weight = 0.1 - (0.05 * sign) * row_a_out[1 - side, pl.ds(0, kk), :]
        for f in (0, 1):
            at = pl.ds((2 + f) * kk * TX + x, kk, stride=TX)
            rows = pl.ds(f * kk, kk)
            jump = jnp.where(wet, row_b_in[side, rows, :] - row_b_out[1 - side, rows, :], 0.0)
            out_ref[at, :] = out_ref[at, :] + weight * jump
    patches = []
    for side, sign in ((0, 1.0), (1, -1.0)):
        wet, jump = faces[side][:2]
        both = jnp.where(in_p, (-0.5 * sign) * jump, jump)
        mine = my_columns[side]
        first = 0.1 * (both + jnp.where(in_v, turn(jnp.where(in_p, both, 0.0), -kk, 1), 0.0))
        v = jnp.where(lane < kk, turn(mine, -kk, 1), mine)
        jump = jnp.where(
            wet,
            col_b_in[side] - col_b_out[1 - side],
            0.0,
        )
        second = (0.1 - (0.05 * sign) * v) * jump
        patch = jnp.where(lane < 2 * kk, first, turn(second, 2 * kk, 1))
        patches.append(patch)
    north, south = turn(patches[0], -1, 1), patches[1]
    odd = lane % 2 == 1
    mixed = [jnp.where(odd, north, south), jnp.where(odd, south, north)]
    outer = jnp.logical_or(lane == 0, lane == TY - 1)

    def patch_columns(i, carry):
        for j in range(2):
            add = pltpu.roll(mixed[j], lax.rem(TY - (2 * i + j), TY), 1)
            at = at_level(2 * i + j)
            out_ref[at, :] = out_ref[at, :] + jnp.where(outer, add, 0.0)
        return carry

    unrolled(2 * kk, 16, patch_columns, 0)

    for x in links_2d + links_relay:
        x.wait_recv()

    def beside(pair, shift):
        c, d = [turn(x, shift, 1) for x in pair]
        edge = iota(c.shape, 1) == (TY - 1 if shift < 0 else 0)
        return jnp.where(edge, d, c), jnp.where(edge, c, d)

    wide = 3 * TX
    edges = jnp.zeros((2, 8, TY), F32)
    for ref in (eta_ref, u_ref, v_ref, lev_ref):
        ref[:, pl.ds(0, 8), :] = edges
        ref[:, pl.ds(8 + wide, 8), :] = edges
    lev_ref[0, pl.ds(8, wide), :] = flat2d[3]
    for j in range(3):
        part = pl.ds(8 + j * TX, TX)
        wet_d = None
        for f, ref in ((3, lev_ref), (0, eta_ref), (1, u_ref), (2, v_ref)):
            q = unpack(rim_in[j, pl.ds(0, TX), :], rim_in[3 + j, pl.ds(0, TX), :], f, lane)
            if f == 3:
                wet_d = q > 0.0
                wet_c = flat2d[3, pl.ds(j * TX, TX), :] > 0.0
                ref[1, part, :] = q
            else:
                ref[0, part, :] = jnp.where(wet_c, flat2d[f, pl.ds(j * TX, TX), :], 0.0)
                ref[1, part, :] = jnp.where(wet_d, q, 0.0)
    for b in range(0, wide, 8):
        at, ahead, behind = [pl.ds(8 + b + d, 8) for d in (0, 1, -1)]
        here = [lev_ref[h, at, :] for h in range(2)]
        norths = beside(here, -1)
        souths = beside(here, 1)
        for h in range(2):
            is_wet = here[h] > 0.0
            others = (lev_ref[h, ahead, :], lev_ref[h, behind, :], norths[h], souths[h])
            faces = [
                jnp.where(jnp.logical_and(is_wet, other > 0.0), 0.15, 0.0) for other in others
            ]
            scale = 1.0 / kk
            planes = [face * (other * scale) for face, other in zip(faces, others)]
            planes.append((faces[0] - faces[1]) * (here[h] * scale))
            planes.append((faces[2] - faces[3]) * (here[h] * scale))
            for n, plane in enumerate(planes + faces):
                coef[n, h, pl.ds(b, 8), :] = plane

    lane_8 = iota((8, TY), 1)
    y_d = lax.rem(gy * TY + lane_8 + jnp.where(lane_8 < TY // 2, TY, -TY) + ny * TY, ny * TY)
    cor = [
        0.15 * (2.0 * ((gy * TY + lane_8).astype(F32) + 0.5) / row_total - 1.0),
        0.15 * (2.0 * (y_d.astype(F32) + 0.5) / row_total - 1.0),
    ]

    meridional_faces(0, [cols_in[0, side] for side in range(2)])
    meridional_faces(2, [cols_in[1, side] for side in range(2)])

    def update_eta(low, high):
        for b in range(low, high, 8):
            at, ahead, behind = [pl.ds(8 + b + d, 8) for d in (0, 1, -1)]
            c_at = pl.ds(b, 8)
            v = [v_ref[h, at, :] for h in range(2)]
            vn = beside(v, -1)
            vs = beside(v, 1)
            for h in range(2):
                c = [coef[n, h, c_at, :] for n in range(6)]
                x = (c[0] * u_ref[h, ahead, :] - c[1] * u_ref[h, behind, :]) + c[4] * u_ref[h, at, :]
                y = (c[2] * vn[h] - c[3] * vs[h]) + c[5] * v[h]
                eta_ref[h, at, :] = eta_ref[h, at, :] - (x + y)

    def update_velocity(low, high, pushed, halves, totals):
        total_u, total_v = [], []
        for b in range(low, high, 8):
            at, ahead, behind = [pl.ds(8 + b + d, 8) for d in (0, 1, -1)]
            c_at = pl.ds(b, 8)
            e = [eta_ref[h, at, :] for h in range(2)]
            en = beside(e, -1)
            es = beside(e, 1)
            for h in range(halves):
                c = [coef[n, h, c_at, :] for n in range(6, 10)]
                gx_eta = c[0] * (eta_ref[h, ahead, :] - e[h]) + c[1] * (e[h] - eta_ref[h, behind, :])
                gy_eta = c[2] * (en[h] - e[h]) + c[3] * (e[h] - es[h])
                u = u_ref[h, at, :]
                v = v_ref[h, at, :]
                add_u = cor[h] * v
                add_v = cor[h] * u
                if pushed:
                    add_u = add_u + push[0, h, c_at, :]
                    add_v = add_v - push[1, h, c_at, :]
                new_u = (u - gx_eta) + add_u
                new_v = (v - gy_eta) - add_v
                u_ref[h, at, :] = new_u
                v_ref[h, at, :] = new_v
                if h == 0 and TX <= b < 2 * TX:
                    total_u.append(new_u)
                    total_v.append(new_v)
        if not pushed:
            return None
        return (
            totals[0] + jnp.concatenate(total_u, axis=0),
            totals[1] + jnp.concatenate(total_v, axis=0),
        )

    update_eta(0, wide)
    update_velocity(0, wide, False, 2, None)
    for x in links_force:
        x.wait_recv()
    for j in range(3):
        for f, ref in ((0, u_ref), (1, v_ref)):
            for h in (0, 1):
                at = j * TX + h * half
                part = pl.ds(at, half)
                inner = pl.ds(8 + at, half)
                beyond = unpack(frim_in[j], frim_in[3 + j], 2 * f + h, lane_h)
                for side, add in ((0, force[f, part, :]), (1, beyond)):
                    add = push[f, side, part, :] + add
                    push[f, side, part, :] = add
                    ref[side, inner, :] = ref[side, inner, :] + add
    totals = (u_ref[0, pl.ds(8 + TX, TX), :], v_ref[0, pl.ds(8 + TX, TX), :])
    per = NSUB // 4
    for step in range(1, NSUB):
        group, i = step // per, step % per
        low, high = 8 * group, wide - 8 * group
        update_eta(low, high)
        if i == per - 1:
            low, high = low + 8, high - 8
        totals = update_velocity(low, high, True, 1 if step == NSUB - 1 else 2, totals)
    total_u, total_v = totals

    for f, ref in enumerate((eta_ref, u_ref, v_ref)):
        baro_out[f] = ref[0, pl.ds(8 + TX, TX), :]
    shift_out[0] = total_u * (1.0 / NSUB) - mean_u
    shift_out[1] = total_v * (1.0 / NSUB) - mean_v
    shift_out[2] = lev
    for x in links_a + links_rim + links_2d + links_b + links_relay + links_force:
        x.wait_send()


def finish(kk, star, baro, shift, out_hbm, baro_hbm, fast, sems):
    half = 2 * kk * TX
    copies = [
        pltpu.make_async_copy(star.at[pl.ds(half, half), :], out_hbm.at[pl.ds(half, half), :], sems.at[0]),
        pltpu.make_async_copy(baro, baro_hbm, sems.at[1]),
    ]
    for x in copies:
        x.start()
    lev = shift[2]
    for f in (0, 1):
        add = shift[f]

        def body(k, carry):
            i = f * kk + k
            fast[at_level(i), :] = jnp.where(k.astype(F32) < lev, star[at_level(i), :] + add, 0.0)
            return carry

        unrolled(kk, 4, body, 0)
        part = pl.ds(f * kk * TX, kk * TX)
        copies.append(pltpu.make_async_copy(fast.at[part, :], out_hbm.at[part, :], sems.at[2 + f]))
        copies[-1].start()
    for x in copies:
        x.wait()


def per_device(ocean_state, barotropic, levels):
    kk = ocean_state.shape[1]
    rows = 4 * kk * TX
    hbm = pl.BlockSpec(memory_space=pltpu.HBM)
    vmem = pl.BlockSpec(memory_space=pltpu.VMEM)
    links = 24

    def shape(*dims):
        return jax.ShapeDtypeStruct(dims, F32)

    star, baro, shift = pl.pallas_call(
        functools.partial(kernel, kk),
        out_shape=tuple(pltpu.VMEM(d, F32) for d in ((rows, TY), (3, TX, TY), (3, TX, TY))),
        in_specs=[hbm] * 3,
        out_specs=(vmem,) * 3,
        scratch_shapes=[
            pltpu.VMEM((rows, TY), F32),
            pltpu.VMEM((kk * TX, TY), F32),
            pltpu.VMEM((TX, TY), jnp.int32),
            pltpu.VMEM((4, 3 * TX, TY), F32),
            pltpu.VMEM((2, 2 * TX, TY), F32),
            pltpu.VMEM((6, 2 * TX, TY), F32),
            pltpu.VMEM((2, 3 * kk + 8, TY), F32),
            pltpu.VMEM((2, 3 * kk + 8, TY), F32),
            pltpu.VMEM((2, 2 * kk, TY), F32),
            pltpu.VMEM((2, 2 * kk, TY), F32),
            pltpu.VMEM((2, 2, TX, TY), F32),
            pltpu.VMEM((2, TX, TY), F32),
            pltpu.VMEM((2, TX, TY), F32),
            pltpu.VMEM((2, 3 * TX, TY), F32),
            pltpu.VMEM((2, 2, 3 * TX, TY), F32),
            pltpu.VMEM((2, TX // 2, TY), F32),
            pltpu.VMEM((6, TX // 2, TY), F32),
            pltpu.VMEM((2, 3 * TX + 16, TY), F32),
            pltpu.VMEM((2, 3 * TX + 16, TY), F32),
            pltpu.VMEM((2, 3 * TX + 16, TY), F32),
            pltpu.VMEM((2, 3 * TX + 16, TY), F32),
            pltpu.VMEM((10, 2, 3 * TX, TY), F32),
            pltpu.SemaphoreType.DMA((3,)),
            pltpu.SemaphoreType.DMA((4 * max(1, kk // MORE),)),
            pltpu.SemaphoreType.DMA((links,)),
            pltpu.SemaphoreType.DMA((links,)),
        ],
        compiler_params=pltpu.CompilerParams(
            collective_id=0, has_side_effects=True, vmem_limit_bytes=32 * 1024 * 1024
        ),
        name="ocean_step",
    )(*[pltpu.with_memory_space_constraint(a, pltpu.HBM) for a in (ocean_state.reshape(rows, TY), barotropic, levels)])
    new, baro = pl.pallas_call(
        functools.partial(finish, kk),
        out_shape=(shape(rows, TY), shape(3, TX, TY)),
        in_specs=[vmem] * 3,
        out_specs=(hbm,) * 2,
        scratch_shapes=[
            pltpu.VMEM((2 * kk * TX, TY), F32),
            pltpu.SemaphoreType.DMA((4,)),
        ],
        compiler_params=pltpu.CompilerParams(vmem_limit_bytes=16 * 1024 * 1024),
        name="finish",
    )(star, baro, shift)
    return new.reshape(ocean_state.shape), baro


def solution(mesh):
    in_specs = (P(None, None, "gx", "gy"), P(None, "gx", "gy"), P("gx", "gy"))
    out_specs = (P(None, None, "gx", "gy"), P(None, "gx", "gy"))
    return jax.shard_map(
        per_device, mesh=mesh, in_specs=in_specs, out_specs=out_specs, check_vma=False
    )
```

```python
import functools

import jax
import jax.numpy as jnp
from jax import lax
from jax.experimental import pallas as pl
from jax.experimental.pallas import tpu as pltpu
from jax.sharding import PartitionSpec as P

MESH = pl.DeviceIdType.MESH
NSUB = 16
TX = 32
TY = 128
RIM = 32
MORE = 8
F32 = jnp.float32


def iota(shape, dim):
    return lax.broadcasted_iota(jnp.int32, shape, dim)


def turn(a, shift, axis):
    return pltpu.roll(a, shift % a.shape[axis], axis)


def at_level(i):
    return pl.ds(pl.multiple_of(i * TX, TX), TX)


def unrolled(n, times, body, carry):
    times = min(n, times)

    def several(o, carry):
        for j in range(times):
            carry = body(o * times + j, carry)
        return carry

    return lax.fori_loop(0, n // times, several, carry)


class Link:
    def __init__(self, copy, sends=None, receives=None):
        self.copy, self.sends, self.receives = copy, sends, receives

    def do(self, what, when):
        if when is None:
            what()
        else:
            pl.when(when)(lambda: what())

    def start(self):
        self.do(self.copy.start, self.sends)

    def wait_send(self):
        self.do(self.copy.wait_send, self.sends)

    def wait_recv(self):
        self.do(self.copy.wait_recv, self.receives)


def pack(parts, lane):
    north, south = parts[3], parts[0]
    for f in range(4):
        if f != 3:
            north = jnp.where(lane // RIM == f, turn(parts[f], RIM * (f + 1), 1), north)
        if f != 0:
            south = jnp.where(lane // RIM == f, turn(parts[f], RIM * f, 1), south)
    return north, south


def unpack(north, south, f, lane):
    a = turn(north, -RIM * f, 1)
    b = turn(south, TY - RIM - RIM * f, 1)
    return jnp.where(lane < RIM, a, jnp.where(lane >= TY - RIM, b, 0.0))


def kernel(
    kk,
    ocean_hbm,
    baro_hbm,
    lev_hbm,
    out_ref,
    baro_out,
    shift_out,
    oc,
    press_ref,
    lev_i,
    flat2d,
    rim_out,
    rim_in,
    row_a_out,
    row_a_in,
    row_b_out,
    row_b_in,
    col_a_out,
    col_a_in,
    cols_in,
    col_b_out,
    col_b_in,
    force,
    push,
    frim_out,
    frim_in,
    eta_ref,
    u_ref,
    v_ref,
    lev_ref,
    coef,
    local_sem,
    load_sem,
    send_sem,
    recv_sem,
):
    gx = lax.axis_index("gx")
    gy = lax.axis_index("gy")
    nx = lax.axis_size("gx")
    ny = lax.axis_size("gy")
    xe = lax.rem(gx + 1, nx)
    xw = lax.rem(gx + nx - 1, nx)
    yn = lax.rem(gy + 1, ny)
    ys = lax.rem(gy + ny - 1, ny)
    has_n = gy < ny - 1
    has_s = gy > 0

    barrier = pltpu.get_barrier_semaphore()

    def greet(x, y):
        pl.semaphore_signal(barrier, inc=1, device_id=(x, y), device_id_type=MESH)

    @pl.when(has_n)
    def _():
        greet(gx, yn)

    @pl.when(has_s)
    def _():
        greet(gx, ys)

    greet(xw, gy)
    greet(xe, gy)
    greeted = 2 + has_n.astype(jnp.int32) + has_s.astype(jnp.int32)

    some = min(kk, MORE)

    def load(c, f):
        part = pl.ds(pl.multiple_of((f * kk + c * some) * TX, TX), some * TX)
        return pltpu.make_async_copy(ocean_hbm.at[part, :], oc.at[part, :], load_sem.at[c * 4 + f])

    load_b = pltpu.make_async_copy(baro_hbm, flat2d.at[pl.ds(0, 3), pl.ds(TX, TX), :], local_sem.at[1])
    load_l = pltpu.make_async_copy(lev_hbm, lev_i, local_sem.at[2])
    load_l.start()
    load_b.start()
    for c in range(kk // some):
        for f in range(4):
            load(c, f).start()

    lane = iota((TX, TY), 1)
    row = iota((TX, TY), 0)
    zero = jnp.zeros((TX, TY), F32)
    counter = [0]

    def link(src, dst, dev, sends=None, receives=None):
        index = counter[0]
        counter[0] += 1
        return Link(
            pltpu.make_async_remote_copy(
                src_ref=src,
                dst_ref=dst,
                send_sem=send_sem.at[index],
                recv_sem=recv_sem.at[index],
                device_id=dev,
                device_id_type=MESH,
            ),
            sends,
            receives,
        )

    def southward(src, dst, x=gx):
        return link(src, dst, (x, ys), has_s, has_n)

    def northward(src, dst, x=gx):
        return link(src, dst, (x, yn), has_n, has_s)

    def westward(src, dst):
        return link(src, dst, (xw, gy))

    def eastward(src, dst):
        return link(src, dst, (xe, gy))

    own = pl.ds(TX, TX)
    after = pl.ds(2 * TX, TX)
    before = pl.ds(0, TX)
    links_a = [
        westward(row_a_out.at[0], row_a_in.at[0]),
        eastward(row_a_out.at[1], row_a_in.at[1]),
    ]
    links_rim = [
        southward(rim_out.at[1], rim_in.at[1]),
        northward(rim_out.at[0], rim_in.at[4]),
    ]
    links_col = [
        southward(col_a_out.at[1], col_a_in.at[1]),
        northward(col_a_out.at[0], col_a_in.at[4]),
    ]
    links_cols = [
        westward(col_a_out, cols_in.at[1]),
        eastward(col_a_out, cols_in.at[0]),
    ]
    links_2d = [
        westward(flat2d.at[:, own, :], flat2d.at[:, after, :]),
        eastward(flat2d.at[:, own, :], flat2d.at[:, before, :]),
    ]
    links_row_b = [
        westward(row_b_out.at[0], row_b_in.at[0]),
        eastward(row_b_out.at[1], row_b_in.at[1]),
    ]
    links_col_b = [
        southward(col_b_out.at[0], col_b_in.at[0]),
        northward(col_b_out.at[1], col_b_in.at[1]),
    ]

    def relay(ref):
        return [
            link(ref.at[1], ref.at[2], (xw, gy), has_n, has_n),
            link(ref.at[1], ref.at[0], (xe, gy), has_n, has_n),
            link(ref.at[4], ref.at[5], (xw, gy), has_s, has_s),
            link(ref.at[4], ref.at[3], (xe, gy), has_s, has_s),
        ]

    links_relay = relay(rim_in)
    links_col_relay = relay(col_a_in)
    links_force = [
        southward(frim_out.at[1], frim_in.at[0], xe),
        northward(frim_out.at[0], frim_in.at[3], xe),
        southward(frim_out.at[1], frim_in.at[2], xw),
        northward(frim_out.at[0], frim_in.at[5], xw),
        southward(frim_out.at[1], frim_in.at[1]),
        northward(frim_out.at[0], frim_in.at[4]),
        westward(force.at[:, own, :], force.at[:, after, :]),
        eastward(force.at[:, own, :], force.at[:, before, :]),
    ]

    @pl.when(jnp.logical_not(has_n))
    def _():
        rim_in[0:3] = jnp.zeros((3, TX, TY), F32)
        col_a_in[0:3] = jnp.zeros((3, TX, TY), F32)
        frim_in[0:3] = jnp.zeros((3, TX // 2, TY), F32)

    @pl.when(jnp.logical_not(has_s))
    def _():
        rim_in[3:6] = jnp.zeros((3, TX, TY), F32)
        col_a_in[3:6] = jnp.zeros((3, TX, TY), F32)
        frim_in[3:6] = jnp.zeros((3, TX // 2, TY), F32)

    load_l.wait()
    lev = lev_i[...].astype(F32)
    flat2d[3, own, :] = lev
    load_b.wait()
    north, south = pack([flat2d[f, own, :] for f in range(4)], lane)
    rim_out[0] = north
    rim_out[1] = south

    for c in range(kk // some):
        for f in range(4):
            load(c, f).wait()
    level = iota((kk, TY), 0).astype(F32)
    for side, x in ((0, 0), (1, TX - 1)):
        row_a_out[side, pl.ds(0, 2 * kk), :] = oc[pl.ds(x, 2 * kk, stride=TX), :]
        t = oc[pl.ds(2 * kk * TX + x, kk, stride=TX), :]
        s = oc[pl.ds(3 * kk * TX + x, kk, stride=TX), :]
        row_b_out[side, pl.ds(0, kk), :] = t
        row_b_out[side, pl.ds(kk, kk), :] = s
        row_a_out[side, pl.ds(3 * kk, 8), :] = jnp.broadcast_to(lev[x : x + 1], (8, TY))
        layers = jnp.where(level < lev[x : x + 1], 0.1 * s - 0.2 * t, 0.0)
        press = jnp.zeros((1, TY), F32)
        for k in range(kk):
            press = press + layers[k : k + 1]
            row_a_out[side, pl.ds(2 * kk + k, 1), :] = press

    pl.semaphore_wait(barrier, greeted)
    for x in links_a + links_rim + links_2d + links_row_b:
        x.start()

    def gather(k, carry):
        press, first_a, last_a, first_b, last_b = carry
        t = oc[at_level(2 * kk + k), :]
        s = oc[at_level(3 * kk + k), :]
        press = press + jnp.where(k.astype(F32) < lev, 0.1 * s - 0.2 * t, 0.0)
        press_ref[at_level(k), :] = press
        u = oc[at_level(k), :]
        v = oc[at_level(kk + k), :]
        for f, q in ((0, u), (1, v), (2, press)):
            moved = pltpu.roll(q, f * kk + k, 1)
            first_a = jnp.where(lane == f * kk + k, moved, first_a)
            last_a = jnp.where(lane == lax.rem(f * kk + k + TY - 1, TY), moved, last_a)
        for f, q in ((0, t), (1, s)):
            moved = pltpu.roll(q, f * kk + k, 1)
            first_b = jnp.where(lane == f * kk + k, moved, first_b)
            last_b = jnp.where(lane == lax.rem(f * kk + k + TY - 1, TY), moved, last_b)
        return press, first_a, last_a, first_b, last_b

    def gather_chunk(c, carry):
        for j in range(some):
            carry = gather(c * some + j, carry)
        return carry

    _, first_a, last_a, first_b, last_b = lax.fori_loop(0, kk // some, gather_chunk, (zero,) * 5)
    last_a = turn(last_a, 1, 1)
    last_b = turn(last_b, 1, 1)
    first_lev = jnp.broadcast_to(lev[:, 0:1], (TX, TY))
    last_lev = jnp.broadcast_to(lev[:, TY - 1 : TY], (TX, TY))
    in_lev = lane >= 96
    col_a_out[0] = jnp.where(in_lev, last_lev, last_a)
    col_a_out[1] = jnp.where(in_lev, first_lev, first_a)
    col_b_out[0] = first_b
    col_b_out[1] = last_b
    for x in links_col + links_cols + links_col_b:
        x.start()

    face_e = jnp.where(row == TX - 1, 0.0, jnp.minimum(lev, turn(lev, -1, 0)))
    face_n = jnp.where(lane == TY - 1, 0.0, jnp.minimum(lev, turn(lev, -1, 1)))
    inverse = 1.0 / jnp.maximum(lev, 1.0)
    row_total = float(ny * TY)
    y_own = (gy * TY + lane).astype(F32)
    fcor = 0.5 * (2.0 * (y_own + 0.5) / row_total - 1.0)

    def jumps(q, in_e, in_n):
        e = jnp.where(in_e, turn(q, -1, 0) - q, 0.0)
        n = jnp.where(in_n, turn(q, -1, 1) - q, 0.0)
        return e, turn(e, 1, 0), n, turn(n, 1, 1)

    def momentum(k, carry):
        sum_u, sum_v, col_u, col_v = carry
        level = k.astype(F32)
        wet = level < lev
        in_e = level < face_e
        in_n = level < face_n
        u = oc[at_level(k), :]
        v = oc[at_level(kk + k), :]
        pe, pw, pn, ps = jumps(press_ref[at_level(k), :], in_e, in_n)
        ue, uw, un, us = jumps(u, in_e, in_n)
        ve, vw, vn, vs = jumps(v, in_e, in_n)
        tend_u = ((ue - uw) + (un - us)) + (fcor * v - 0.5 * (pe + pw))
        tend_v = ((ve - vw) + (vn - vs)) - (fcor * u + 0.5 * (pn + ps))
        star_u = u + 0.1 * tend_u
        star_v = v + 0.1 * tend_v
        out_ref[at_level(k), :] = star_u
        out_ref[at_level(kk + k), :] = star_v
        return (
            sum_u + jnp.where(wet, tend_u, 0.0),
            sum_v + jnp.where(wet, tend_v, 0.0),
            col_u + jnp.where(wet, star_u, 0.0),
            col_v + jnp.where(wet, star_v, 0.0),
        )

    def tracers(k, carry):
        level = k.astype(F32)
        wet = level < lev
        in_e = level < face_e
        in_n = level < face_n
        u = 0.05 * oc[at_level(k), :]
        v = 0.05 * oc[at_level(kk + k), :]
        for f in (2, 3):
            q = oc[at_level(f * kk + k), :]
            e, w, n, s = jumps(q, in_e, in_n)
            new = q + (0.1 * ((e - w) + (n - s)) - (u * (e + w) + v * (n + s)))
            out_ref[at_level(f * kk + k), :] = jnp.where(wet, new, 0.0)
        return carry

    sum_u, sum_v, col_u, col_v = unrolled(kk, 4, momentum, (zero,) * 4)

    for x in links_a:
        x.wait_recv()
    rows_add = []
    for side, sign in ((0, 1.0), (1, -1.0)):
        mine = row_a_out.at[1 - side]
        theirs = row_a_in.at[side]
        face = jnp.minimum(mine[pl.ds(3 * kk, 1), :], theirs[pl.ds(3 * kk, 1), :])
        wet = level < face
        ju, jv, jp = [
            jnp.where(wet, theirs[pl.ds(f * kk, kk), :] - mine[pl.ds(f * kk, kk), :], 0.0)
            for f in range(3)
        ]
        rows_add.append((wet, ju - (0.5 * sign) * jp, jv))

    def total(a):
        return jnp.sum(a, axis=0, keepdims=True)

    zonal_u = jnp.where(row == TX - 1, total(rows_add[0][1]), 0.0)
    zonal_u += jnp.where(row == 0, total(rows_add[1][1]), 0.0)
    zonal_v = jnp.where(row == TX - 1, total(rows_add[0][2]), 0.0)
    zonal_v += jnp.where(row == 0, total(rows_add[1][2]), 0.0)
    force_u = (sum_u + zonal_u) * (0.3 * inverse)
    force_v = (sum_v + zonal_v) * (0.3 * inverse)
    force[0, own, :] = force_u
    force[1, own, :] = force_v
    half = TX // 2
    lane_h = iota((half, TY), 1)
    north, south = pack(
        [a[h * half : (h + 1) * half] for a in (force_u, force_v) for h in (0, 1)], lane_h
    )
    frim_out[0] = north
    frim_out[1] = south
    for x in links_force:
        x.start()

    for x in links_rim:
        x.wait_recv()
    for x in links_relay:
        x.start()
    unrolled(kk, MORE, tracers, 0)
    for x in links_col:
        x.wait_recv()
    for x in links_col_relay:
        x.start()

    level_l = jnp.where(lane < kk, lane, jnp.where(lane < 2 * kk, lane - kk, lane - 2 * kk)).astype(F32)
    in_u = lane < kk
    in_v = jnp.logical_and(lane >= kk, lane < 2 * kk)
    in_p = jnp.logical_and(lane >= 2 * kk, lane < 3 * kk)

    def across(a, mask):
        return jnp.sum(jnp.where(mask, a, 0.0), axis=1, keepdims=True)

    def meridional_face(side, mine, theirs):
        sign = (1.0, -1.0)[side]
        near, far = (TY - 1, 0) if side == 0 else (0, TY - 1)
        my_lev, their_lev = [jnp.broadcast_to(a[:, TY - 1 : TY], (TX, TY)) for a in (mine, theirs)]
        wet = level_l < jnp.minimum(my_lev, their_lev)
        jump = jnp.where(wet, theirs - mine, 0.0)
        jump_u = across(jump, in_u)
        jump_v = across(jump, in_v)
        jump_p = (0.5 * sign) * across(jump, in_p)
        here = [jnp.where(lane == near, a, 0.0) for a in (jump_u, jump_v - jump_p)]
        there = [jnp.where(lane == far, a, 0.0) for a in (-jump_u, -jump_v - jump_p)]
        scale = [0.3 / jnp.maximum(a, 1.0) for a in (my_lev, their_lev)]
        return wet, jump, here, [a * scale[0] for a in here], [a * scale[1] for a in there]

    def meridional_faces(j, mine):
        faces = [
            meridional_face(side, mine[side], col_a_in[3 * side + j])
            for side in range(2)
        ]
        for f in range(2):
            push[f, 0, pl.ds(j * TX, TX), :] = faces[0][3][f] + faces[1][3][f]
            push[f, 1, pl.ds(j * TX, TX), :] = faces[0][4][f] + faces[1][4][f]
        return faces

    my_columns = [col_a_out[side] for side in range(2)]
    faces = meridional_faces(1, my_columns)
    mean_u = (col_u + 0.1 * (zonal_u + faces[0][2][0] + faces[1][2][0])) * inverse
    mean_v = (col_v + 0.1 * (zonal_v + faces[0][2][1] + faces[1][2][1])) * inverse

    for x in links_row_b + links_col_b:
        x.wait_recv()
    for side, sign, x in ((0, 1.0, TX - 1), (1, -1.0, 0)):
        wet, add_u, add_v = rows_add[side]
        for f, add in ((0, add_u), (1, add_v)):
            at = pl.ds(f * kk * TX + x, kk, stride=TX)
            out_ref[at, :] = out_ref[at, :] + 0.1 * add
        weight = 0.1 - (0.05 * sign) * row_a_out[1 - side, pl.ds(0, kk), :]
        for f in (0, 1):
            at = pl.ds((2 + f) * kk * TX + x, kk, stride=TX)
            rows = pl.ds(f * kk, kk)
            jump = jnp.where(wet, row_b_in[side, rows, :] - row_b_out[1 - side, rows, :], 0.0)
            out_ref[at, :] = out_ref[at, :] + weight * jump
    patches = []
    for side, sign in ((0, 1.0), (1, -1.0)):
        wet, jump = faces[side][:2]
        both = jnp.where(in_p, (-0.5 * sign) * jump, jump)
        mine = my_columns[side]
        first = 0.1 * (both + jnp.where(in_v, turn(jnp.where(in_p, both, 0.0), -kk, 1), 0.0))
        v = jnp.where(lane < kk, turn(mine, -kk, 1), mine)
        jump = jnp.where(
            wet,
            col_b_in[side] - col_b_out[1 - side],
            0.0,
        )
        second = (0.1 - (0.05 * sign) * v) * jump
        patch = jnp.where(lane < 2 * kk, first, turn(second, 2 * kk, 1))
        patches.append(patch)
    north, south = turn(patches[0], -1, 1), patches[1]
    odd = lane % 2 == 1
    mixed = [jnp.where(odd, north, south), jnp.where(odd, south, north)]
    outer = jnp.logical_or(lane == 0, lane == TY - 1)

    def patch_columns(i, carry):
        for j in range(2):
            add = pltpu.roll(mixed[j], lax.rem(TY - (2 * i + j), TY), 1)
            at = at_level(2 * i + j)
            out_ref[at, :] = out_ref[at, :] + jnp.where(outer, add, 0.0)
        return carry

    unrolled(2 * kk, 16, patch_columns, 0)

    for x in links_2d + links_relay:
        x.wait_recv()

    def beside(pair, shift):
        c, d = [turn(x, shift, 1) for x in pair]
        edge = iota(c.shape, 1) == (TY - 1 if shift < 0 else 0)
        return jnp.where(edge, d, c), jnp.where(edge, c, d)

    wide = 3 * TX
    edges = jnp.zeros((2, 8, TY), F32)
    for ref in (eta_ref, u_ref, v_ref, lev_ref):
        ref[:, pl.ds(0, 8), :] = edges
        ref[:, pl.ds(8 + wide, 8), :] = edges
    lev_ref[0, pl.ds(8, wide), :] = flat2d[3]
    for j in range(3):
        part = pl.ds(8 + j * TX, TX)
        wet_d = None
        for f, ref in ((3, lev_ref), (0, eta_ref), (1, u_ref), (2, v_ref)):
            q = unpack(rim_in[j], rim_in[3 + j], f, lane)
            if f == 3:
                wet_d = q > 0.0
                wet_c = flat2d[3, pl.ds(j * TX, TX), :] > 0.0
                ref[1, part, :] = q
            else:
                ref[0, part, :] = jnp.where(wet_c, flat2d[f, pl.ds(j * TX, TX), :], 0.0)
                ref[1, part, :] = jnp.where(wet_d, q, 0.0)
    for b in range(0, wide, 8):
        at, ahead, behind = [pl.ds(8 + b + d, 8) for d in (0, 1, -1)]
        here = [lev_ref[h, at, :] for h in range(2)]
        norths = beside(here, -1)
        souths = beside(here, 1)
        for h in range(2):
            is_wet = here[h] > 0.0
            others = (lev_ref[h, ahead, :], lev_ref[h, behind, :], norths[h], souths[h])
            faces = [
                jnp.where(jnp.logical_and(is_wet, other > 0.0), 0.15, 0.0) for other in others
            ]
            scale = 1.0 / kk
            planes = [face * (other * scale) for face, other in zip(faces, others)]
            planes.append((faces[0] - faces[1]) * (here[h] * scale))
            planes.append((faces[2] - faces[3]) * (here[h] * scale))
            for n, plane in enumerate(planes + faces):
                coef[n, h, pl.ds(b, 8), :] = plane

    lane_8 = iota((8, TY), 1)
    y_d = lax.rem(gy * TY + lane_8 + jnp.where(lane_8 < TY // 2, TY, -TY) + ny * TY, ny * TY)
    cor = [
        0.15 * (2.0 * ((gy * TY + lane_8).astype(F32) + 0.5) / row_total - 1.0),
        0.15 * (2.0 * (y_d.astype(F32) + 0.5) / row_total - 1.0),
    ]

    def update_eta(low, high):
        for b in range(low, high, 8):
            at, ahead, behind = [pl.ds(8 + b + d, 8) for d in (0, 1, -1)]
            c_at = pl.ds(b, 8)
            v = [v_ref[h, at, :] for h in range(2)]
            vn = beside(v, -1)
            vs = beside(v, 1)
            for h in range(2):
                c = [coef[n, h, c_at, :] for n in range(6)]
                x = (c[0] * u_ref[h, ahead, :] - c[1] * u_ref[h, behind, :]) + c[4] * u_ref[h, at, :]
                y = (c[2] * vn[h] - c[3] * vs[h]) + c[5] * v[h]
                eta_ref[h, at, :] = eta_ref[h, at, :] - (x + y)

    def update_velocity(low, high, pushed, halves, totals):
        total_u, total_v = [], []
        for b in range(low, high, 8):
            at, ahead, behind = [pl.ds(8 + b + d, 8) for d in (0, 1, -1)]
            c_at = pl.ds(b, 8)
            e = [eta_ref[h, at, :] for h in range(2)]
            en = beside(e, -1)
            es = beside(e, 1)
            for h in range(halves):
                c = [coef[n, h, c_at, :] for n in range(6, 10)]
                gx_eta = c[0] * (eta_ref[h, ahead, :] - e[h]) + c[1] * (e[h] - eta_ref[h, behind, :])
                gy_eta = c[2] * (en[h] - e[h]) + c[3] * (e[h] - es[h])
                u = u_ref[h, at, :]
                v = v_ref[h, at, :]
                add_u = cor[h] * v
                add_v = cor[h] * u
                if pushed:
                    add_u = add_u + push[0, h, c_at, :]
                    add_v = add_v - push[1, h, c_at, :]
                new_u = (u - gx_eta) + add_u
                new_v = (v - gy_eta) - add_v
                u_ref[h, at, :] = new_u
                v_ref[h, at, :] = new_v
                if h == 0 and TX <= b < 2 * TX:
                    total_u.append(new_u)
                    total_v.append(new_v)
        if not pushed:
            return None
        return (
            totals[0] + jnp.concatenate(total_u, axis=0),
            totals[1] + jnp.concatenate(total_v, axis=0),
        )

    update_eta(0, wide)
    update_velocity(0, wide, False, 2, None)
    for x in links_cols + links_col_relay:
        x.wait_recv()
    meridional_faces(0, [cols_in[0, side] for side in range(2)])
    meridional_faces(2, [cols_in[1, side] for side in range(2)])
    for x in links_force:
        x.wait_recv()
    for j in range(3):
        for f, ref in ((0, u_ref), (1, v_ref)):
            for h in (0, 1):
                at = j * TX + h * half
                part = pl.ds(at, half)
                inner = pl.ds(8 + at, half)
                beyond = unpack(frim_in[j], frim_in[3 + j], 2 * f + h, lane_h)
                for side, add in ((0, force[f, part, :]), (1, beyond)):
                    add = push[f, side, part, :] + add
                    push[f, side, part, :] = add
                    ref[side, inner, :] = ref[side, inner, :] + add
    totals = (u_ref[0, pl.ds(8 + TX, TX), :], v_ref[0, pl.ds(8 + TX, TX), :])
    per = NSUB // 4
    for step in range(1, NSUB):
        group, i = step // per, step % per
        low, high = 8 * group, wide - 8 * group
        update_eta(low, high)
        if i == per - 1:
            low, high = low + 8, high - 8
        totals = update_velocity(low, high, True, 1 if step == NSUB - 1 else 2, totals)
    total_u, total_v = totals

    for f, ref in enumerate((eta_ref, u_ref, v_ref)):
        baro_out[f] = ref[0, pl.ds(8 + TX, TX), :]
    shift_out[0] = total_u * (1.0 / NSUB) - mean_u
    shift_out[1] = total_v * (1.0 / NSUB) - mean_v
    shift_out[2] = lev
    every = links_a + links_rim + links_2d + links_row_b + links_col + links_cols + links_col_b
    for x in every + links_relay + links_col_relay + links_force:
        x.wait_send()


def finish(kk, star, baro, shift, out_hbm, baro_hbm, fast, sems):
    half = 2 * kk * TX
    copies = [
        pltpu.make_async_copy(star.at[pl.ds(half, half), :], out_hbm.at[pl.ds(half, half), :], sems.at[0]),
        pltpu.make_async_copy(baro, baro_hbm, sems.at[1]),
    ]
    for x in copies:
        x.start()
    lev = shift[2]
    for f in (0, 1):
        add = shift[f]

        def body(k, carry):
            i = f * kk + k
            fast[at_level(i), :] = jnp.where(k.astype(F32) < lev, star[at_level(i), :] + add, 0.0)
            return carry

        unrolled(kk, 4, body, 0)
        part = pl.ds(f * kk * TX, kk * TX)
        copies.append(pltpu.make_async_copy(fast.at[part, :], out_hbm.at[part, :], sems.at[2 + f]))
        copies[-1].start()
    for x in copies:
        x.wait()


def per_device(ocean_state, barotropic, levels):
    kk = ocean_state.shape[1]
    rows = 4 * kk * TX
    hbm = pl.BlockSpec(memory_space=pltpu.HBM)
    vmem = pl.BlockSpec(memory_space=pltpu.VMEM)
    links = 32

    def shape(*dims):
        return jax.ShapeDtypeStruct(dims, F32)

    star, baro, shift = pl.pallas_call(
        functools.partial(kernel, kk),
        out_shape=tuple(pltpu.VMEM(d, F32) for d in ((rows, TY), (3, TX, TY), (3, TX, TY))),
        in_specs=[hbm] * 3,
        out_specs=(vmem,) * 3,
        scratch_shapes=[
            pltpu.VMEM((rows, TY), F32),
            pltpu.VMEM((kk * TX, TY), F32),
            pltpu.VMEM((TX, TY), jnp.int32),
            pltpu.VMEM((4, 3 * TX, TY), F32),
            pltpu.VMEM((2, TX, TY), F32),
            pltpu.VMEM((6, TX, TY), F32),
            pltpu.VMEM((2, 3 * kk + 8, TY), F32),
            pltpu.VMEM((2, 3 * kk + 8, TY), F32),
            pltpu.VMEM((2, 2 * kk, TY), F32),
            pltpu.VMEM((2, 2 * kk, TY), F32),
            pltpu.VMEM((2, TX, TY), F32),
            pltpu.VMEM((6, TX, TY), F32),
            pltpu.VMEM((2, 2, TX, TY), F32),
            pltpu.VMEM((2, TX, TY), F32),
            pltpu.VMEM((2, TX, TY), F32),
            pltpu.VMEM((2, 3 * TX, TY), F32),
            pltpu.VMEM((2, 2, 3 * TX, TY), F32),
            pltpu.VMEM((2, TX // 2, TY), F32),
            pltpu.VMEM((6, TX // 2, TY), F32),
            pltpu.VMEM((2, 3 * TX + 16, TY), F32),
            pltpu.VMEM((2, 3 * TX + 16, TY), F32),
            pltpu.VMEM((2, 3 * TX + 16, TY), F32),
            pltpu.VMEM((2, 3 * TX + 16, TY), F32),
            pltpu.VMEM((10, 2, 3 * TX, TY), F32),
            pltpu.SemaphoreType.DMA((3,)),
            pltpu.SemaphoreType.DMA((4 * max(1, kk // MORE),)),
            pltpu.SemaphoreType.DMA((links,)),
            pltpu.SemaphoreType.DMA((links,)),
        ],
        compiler_params=pltpu.CompilerParams(
            collective_id=0, has_side_effects=True, vmem_limit_bytes=32 * 1024 * 1024
        ),
        name="ocean_step",
    )(*[pltpu.with_memory_space_constraint(a, pltpu.HBM) for a in (ocean_state.reshape(rows, TY), barotropic, levels)])
    new, baro = pl.pallas_call(
        functools.partial(finish, kk),
        out_shape=(shape(rows, TY), shape(3, TX, TY)),
        in_specs=[vmem] * 3,
        out_specs=(hbm,) * 2,
        scratch_shapes=[
            pltpu.VMEM((2 * kk * TX, TY), F32),
            pltpu.SemaphoreType.DMA((4,)),
        ],
        compiler_params=pltpu.CompilerParams(vmem_limit_bytes=16 * 1024 * 1024),
        name="finish",
    )(star, baro, shift)
    return new.reshape(ocean_state.shape), baro


def solution(mesh):
    in_specs = (P(None, None, "gx", "gy"), P(None, "gx", "gy"), P("gx", "gy"))
    out_specs = (P(None, None, "gx", "gy"), P(None, "gx", "gy"))
    return jax.shard_map(
        per_device, mesh=mesh, in_specs=in_specs, out_specs=out_specs, check_vma=False
    )
```
